256 devices in a mesh: team: 4 (over x), row: 8 (over z), col: 8 (over y, core).
Axes of the slice: x: 4, y: 4, z: 8, core: 2. Of those that a mesh axis runs over, the one named last changes fastest.
Arguments:
- child_inverse: bfloat16 [4, 8192, 8192], P('team', 'row', 'col'), may hold values from -0.125 to 0.125
- child_lower: bfloat16 [4, 8192, 8192], P('team', 'row', 'col'), may hold values from -0.0625 to 0.0625
- child_rhs: bfloat16 [4, 8192, 256], P('team', 'col'), may hold values from -6 to 6
- child_diag: float32 [4, 8192], P('team', 'row'), may hold values from -4 to 4, as said below
- child_off: float32 [4, 8192], P('team', 'row'), may hold values from -4 to 4
- child_pattern: int32 [4, 8192], P('team', 'row'), may hold values from 0 to 2, as said below
- child_pivots: int32 [4], P('team'), may hold values from 4096 to 8192, as said below
- child_map: int32 [4, 8192], P('team', 'col'), may hold values from 0 to 16383, as said below
- root_inverse: bfloat16 [16384, 16384], P('row', ('team', 'col')), may hold values from -0.09375 to 0.09375
- root_rhs: bfloat16 [16384, 256], P(('team', 'col')), may hold values from -6 to 6
- root_diag: float32 [16384], P('row'), may hold values from -4 to 4, as said below
- root_off: float32 [16384], P('row'), may hold values from -4 to 4
- root_pattern: int32 [16384], P('row'), may hold values from 0 to 2, as said below
Outputs:
- child_solution: float32 [4, 8192, 256], P('team', 'col')
- root_solution: float32 [16384, 256], P(('team', 'col'))
The draws below stay inside these ranges and needn't reach their ends.
Inputs may be any that keep to these rules, and one draw needn't show every extreme that they name: `child_pivots`: one child has exactly 8192 live pivot rows. `child_pattern`: rows come in aligned pairs: (1, 2) marks a 2x2 pivot block, (0, 0) two 1x1 blocks. `root_pattern`: rows come in aligned pairs: (1, 2) marks a 2x2 pivot block, (0, 0) two 1x1 blocks. `child_diag`: magnitudes lie between 1 and 4, signs vary; the two diagonal entries of a 2x2 pivot block have opposite signs. `root_diag`: magnitudes lie between 1 and 4, signs vary; the two diagonal entries of a 2x2 pivot block have opposite signs. `child_map`: within one child the 8192 entries are distinct. With parent rows taken in aligned blocks of 512, every aligned block of 1024 entries of a child has at most 64 entries in any one parent block, and exactly 64 in some parent block.
All inputs are finite; a program needn't handle non-finite values.
Results may differ from the reference program's by a relative error of at most 0.013.
Values may be sent and summed in bfloat16 or wider, within the bound.
A program may use at most 64 MiB of HBM per device.

```python
import jax
import jax.numpy as jnp
from jax import lax

PC = 8192
UC = 8192
FR = 16384
R = 256
CHILDREN = 4
TARGETS = 32
UPD_BLOCK = 1024
CAPACITY = 64
ROOT_BLOCK = 512
N_COL = 8


def pair_pattern(key, count, length):
    paired = jax.random.randint(key, (count, length // 2), 0, 2)
    return jnp.stack([paired, 2 * paired], axis=-1).reshape(count, length).astype(jnp.int32)


def draw_child_pattern(key, part):
    key = jax.random.fold_in(key, 11)
    return pair_pattern(key, CHILDREN, PC)


def draw_root_pattern(key, part):
    key = jax.random.fold_in(key, 12)
    return pair_pattern(key, 1, FR)[0]


def draw_child_pivots(key, part):
    key = jax.random.fold_in(key, 13)
    first_key, second_key = jax.random.split(key)
    counts = jax.random.randint(first_key, (CHILDREN,), PC // 2, PC + 1)
    chosen = jax.random.randint(second_key, (), 0, CHILDREN)
    return jnp.where(jnp.arange(CHILDREN) == chosen, PC, counts).astype(jnp.int32)


def paired_signs(sign_key, pattern, count, length):
    raw = jnp.where(jax.random.randint(sign_key, (count, length), 0, 2) == 1, 1.0, -1.0)
    pairs = raw.reshape(count, length // 2, 2)
    paired = pattern.reshape(count, length // 2, 2)[:, :, 0] == 1
    second = jnp.where(paired, -pairs[:, :, 0], pairs[:, :, 1])
    return jnp.stack([pairs[:, :, 0], second], axis=-1).reshape(count, length)


def draw_child_diag(key, part):
    pattern = pair_pattern(jax.random.fold_in(key, 11), CHILDREN, PC)
    key = jax.random.fold_in(key, 14)
    sign_key, size_key = jax.random.split(key)
    signs = paired_signs(sign_key, pattern, CHILDREN, PC)
    sizes = jnp.exp(jax.random.uniform(size_key, (CHILDREN, PC), jnp.float32, 0.0, jnp.log(4.0)))
    return (signs * sizes).astype(jnp.float32)


def draw_root_diag(key, part):
    pattern = pair_pattern(jax.random.fold_in(key, 12), 1, FR)
    key = jax.random.fold_in(key, 15)
    sign_key, size_key = jax.random.split(key)
    signs = paired_signs(sign_key, pattern, 1, FR)[0]
    sizes = jnp.exp(jax.random.uniform(size_key, (FR,), jnp.float32, 0.0, jnp.log(4.0)))
    return (signs * sizes).astype(jnp.float32)


def block_owners(key):
    first_key, second_key, third_key = jax.random.split(key, 3)
    leading = jax.random.randint(first_key, (), 0, TARGETS)
    others = (leading + 1 + jnp.arange((TARGETS - 1) * CAPACITY) // CAPACITY) % TARGETS
    shuffled = others[jax.random.permutation(second_key, (TARGETS - 1) * CAPACITY)]
    chosen = jnp.concatenate([jnp.full((CAPACITY,), leading, jnp.int32), shuffled[:UPD_BLOCK - CAPACITY].astype(jnp.int32)])
    owners = chosen[jax.random.permutation(third_key, UPD_BLOCK)]
    onehot = (owners[:, None] == jnp.arange(TARGETS)[None, :]).astype(jnp.int32)
    ranks = jnp.sum((jnp.cumsum(onehot, axis=0) - 1) * onehot, axis=1)
    return (owners, ranks)


def draw_child_map(key, part):
    key = jax.random.fold_in(key, 16)
    owner_key, order_key = jax.random.split(key)
    owner_keys = jax.random.split(owner_key, CHILDREN * N_COL)
    owners, ranks = jax.vmap(block_owners)(owner_keys)
    owners = owners.reshape(CHILDREN, N_COL, UPD_BLOCK)
    ranks = ranks.reshape(CHILDREN, N_COL, UPD_BLOCK)
    order_keys = jax.random.split(order_key, CHILDREN * TARGETS)
    orders = jax.vmap(lambda single: jax.random.permutation(single, ROOT_BLOCK))(order_keys).reshape(CHILDREN, TARGETS, ROOT_BLOCK)
    positions = jnp.arange(N_COL)[None, :, None] * CAPACITY + ranks
    child_ids = jnp.broadcast_to(jnp.arange(CHILDREN)[:, None, None], owners.shape)
    offsets = orders[child_ids, owners, positions]
    return (owners * ROOT_BLOCK + offsets).reshape(CHILDREN, UC).astype(jnp.int32)


def shard_levels(rng, shape, cuts, least, high):
    factor_of, own = 1.0, jax.random.fold_in(rng, 6)
    for dim, parts in cuts:
        steps = jnp.exp(jax.random.uniform(jax.random.fold_in(own, dim), (parts,), jnp.float32, least / len(cuts), high / len(cuts)))
        factor_of = factor_of * jnp.repeat(steps, shape[dim] // parts).reshape([-1 if axis == dim else 1 for axis in range(len(shape))])
    return factor_of


def bell_draw(key, dims, spread, reach, shards=(), kind=jnp.bfloat16):
    result = jax.random.normal(key, dims, jnp.float32) * spread
    if len(shards) > 0:
        result = shard_levels(key, dims, shards, -0.22, 0.18) * result
    return jnp.clip(result, min=-reach, max=reach).astype(kind)


def setup_inputs(seed: int = 0) -> dict:
    key_of = jax.random.split(jax.random.key(seed), 14)
    child_inverse = bell_draw(key_of[0], (CHILDREN, PC, PC), (PC // 4) ** -0.5, 0.125, ((0, 4), (1, 8), (2, 8)))
    child_lower = bell_draw(key_of[1], (CHILDREN, PC, UC), PC ** -0.5, 0.0625, ((0, 4), (1, 8), (2, 8)))
    child_rhs = bell_draw(key_of[2], (CHILDREN, PC, R), 1.0, 6.0, ((0, 4), (1, 8)))
    child_diag = draw_child_diag(jax.random.fold_in(key_of[13], 71), 0)
    child_off = jnp.clip(jax.random.uniform(key_of[4], (CHILDREN, PC), jnp.float32, -4.0, 4.0) * shard_levels(key_of[4], (CHILDREN, PC), ((0, 4), (1, 8)), -0.4, 0.0), -4.0, 4.0)
    child_pattern = draw_child_pattern(jax.random.fold_in(key_of[13], 71), 0)
    child_pivots = draw_child_pivots(jax.random.fold_in(key_of[13], 71), 0)
    child_map = draw_child_map(jax.random.fold_in(key_of[13], 71), 0)
    root_inverse = bell_draw(key_of[8], (FR, FR), (FR // 4) ** -0.5, 0.09375, ((0, 8), (1, 32)))
    root_rhs = bell_draw(key_of[9], (FR, R), 1.0, 6.0, ((0, 32),))
    root_diag = draw_root_diag(jax.random.fold_in(key_of[13], 71), 0)
    root_off = jnp.clip(jax.random.uniform(key_of[11], (FR,), jnp.float32, -4.0, 4.0) * shard_levels(key_of[11], (FR,), ((0, 8),), -0.4, 0.0), -4.0, 4.0)
    root_pattern = draw_root_pattern(jax.random.fold_in(key_of[13], 71), 0)
    return dict(child_inverse=child_inverse, child_lower=child_lower, child_rhs=child_rhs, child_diag=child_diag, child_off=child_off, child_pattern=child_pattern, child_pivots=child_pivots, child_map=child_map, root_inverse=root_inverse, root_rhs=root_rhs, root_diag=root_diag, root_off=root_off, root_pattern=root_pattern)


def pivot_solve(values, diagonal, offdiag, pattern):
    first_rows = values[0::2]
    second_rows = values[1::2]
    lead_diag = diagonal[0::2][:, None]
    next_diag = diagonal[1::2][:, None]
    coupling = jnp.where(pattern[0::2] == 1, offdiag[0::2], jnp.zeros_like(offdiag[0::2]))[:, None]
    determinant = lead_diag * next_diag - coupling * coupling
    solved_first = (next_diag * first_rows - coupling * second_rows) / determinant
    solved_second = (lead_diag * second_rows - coupling * first_rows) / determinant
    return jnp.stack([solved_first, solved_second], axis=1).reshape(values.shape)


def forward_apply(matrix, vector):
    return jnp.dot(jnp.tril(matrix, -1), vector, preferred_element_type=jnp.float32) + vector.astype(jnp.float32)


def backward_apply(matrix, vector):
    product = lax.dot_general(jnp.tril(matrix, -1), vector, (((0,), (0,)), ((), ())), preferred_element_type=jnp.float32)
    return product + vector.astype(jnp.float32)


def reference(child_inverse, child_lower, child_rhs, child_diag, child_off, child_pattern, child_pivots, child_map, root_inverse, root_rhs, root_diag, root_off, root_pattern):
    row_ids = jnp.arange(PC, dtype=jnp.int32)

    def child_down(operands):
        inverse_part, lower_part, rhs_part, diagonal, offdiag, pattern, pivots = operands
        live_rows = row_ids < pivots
        solved = jnp.where(live_rows[:, None], forward_apply(inverse_part, rhs_part), jnp.float32(0.0)).astype(jnp.bfloat16)
        scaled = pivot_solve(solved.astype(jnp.float32), diagonal, offdiag, pattern)
        contrib = lax.dot_general(lower_part, solved, (((0,), (0,)), ((), ())), preferred_element_type=jnp.float32)
        return scaled, contrib

    scaled_all, contrib_all = lax.map(child_down, (child_inverse, child_lower, child_rhs, child_diag, child_off, child_pattern, child_pivots))
    assembled = jnp.zeros((FR, R), jnp.float32)
    for child_index in range(CHILDREN):
        assembled = assembled.at[child_map[child_index]].add(contrib_all[child_index])
    updated = (root_rhs.astype(jnp.float32) - assembled).astype(jnp.bfloat16)
    root_scaled = pivot_solve(forward_apply(root_inverse, updated), root_diag, root_off, root_pattern).astype(jnp.bfloat16)
    root_solution = backward_apply(root_inverse, root_scaled)
    root_rounded = root_solution.astype(jnp.bfloat16)

    def child_up(operands):
        inverse_part, lower_part, scaled, mapping, pivots = operands
        live_rows = row_ids < pivots
        fetched = jnp.take(root_rounded, mapping, axis=0)
        remaining = scaled - jnp.dot(lower_part, fetched, preferred_element_type=jnp.float32)
        residual = jnp.where(live_rows[:, None], remaining, jnp.float32(0.0)).astype(jnp.bfloat16)
        return backward_apply(inverse_part, residual)

    child_solution = lax.map(child_up, (child_inverse, child_lower, scaled_all, child_map, child_pivots))
    return child_solution, root_solution
```

```python
import functools

import jax
import jax.numpy as jnp
from jax import lax
from jax.experimental import pallas as pl
from jax.experimental.pallas import tpu as pltpu
from jax.sharding import PartitionSpec as P

BF = jnp.bfloat16
F32 = jnp.float32
MESH = pl.DeviceIdType.MESH
CORES = 2
CAP = 64
TILE = 256
CHAINS = 2


def nn(a, b):
    return jnp.dot(a, b, preferred_element_type=F32)


def nt(a, b):
    return lax.dot_general(a, b, (((1,), (1,)), ((), ())), preferred_element_type=F32)


def body(dims, *refs):
    T, Z, Y, CR, CC, U, RB, RR, R, H = dims
    C = Y * CORES
    Q = T * C
    G = T * Y
    W = R // H
    NS = Q * CAP
    pc, pr, pz, pu = CR // C, RR // Q, RB // Z, CC // Z
    it = iter(refs)
    take = lambda n: [next(it) for _ in range(n)]
    inv_h, low_h, root_h, rhs_h, rrhs_h = take(5)
    cdiag, coff, cpat, rdiag, roff, rpat, cmap, piv = take(8)
    out_c, out_r = take(2)
    inv, invt, low, lst, ls, sel, root, roott, asm, asmt, ident, rhs, rrhs = take(13)
    slot, msend, mrecv, cfa, cfb, rfa, rfb, scaled = take(8)
    s1, r1, s2, r2, sol, s3, r3, s4, r4, upd = take(10)
    s6, r6, s6b, r6b, rsc, s8, r8, rs, s10, r10 = take(10)
    s11, r11, s11b, r11b, res, s13, r13, cs = take(8)
    in_sem, snd, rcv, ysem, msem = take(5)

    t = lax.axis_index("team")
    r = lax.axis_index("row")
    c = lax.axis_index("col")
    y = c // CORES
    k = c % CORES
    me = t * C + c
    sib = (t, r, y * CORES + (1 - k))

    def plane_id(q):
        return (t * 0 + q // C, r, q % C)

    def z_id(d):
        return (t, (r + d) % Z, c)

    def y_id(d):
        return (t, r, ((y + d) % Y) * CORES + k)

    def g_id(g):
        return (g // Y, r, (g % Y) * CORES + k)

    barrier = pltpu.get_barrier_semaphore()

    def greet_plane(d, carry):
        pl.semaphore_signal(barrier, inc=1, device_id=plane_id((me + d) % Q), device_id_type=MESH)
        return carry

    def greet_z(d, carry):
        pl.semaphore_signal(barrier, inc=1, device_id=z_id(d), device_id_type=MESH)
        return carry

    loads = [pltpu.make_async_copy(rhs_h, rhs, in_sem.at[0])]
    for kk in range(CORES):
        loads.append(pltpu.make_async_copy(inv_h.at[:, kk], inv.at[pl.ds(kk * Y, Y)], in_sem.at[1 + kk]))
    for kk in range(CORES):
        loads.append(pltpu.make_async_copy(low_h.at[:, kk], low.at[pl.ds(kk * Y, Y)], in_sem.at[3 + kk]))
    for kk in range(CORES):
        loads.append(pltpu.make_async_copy(root_h.at[:, kk], root.at[pl.ds(kk * G, G)], in_sem.at[5 + kk]))
    loads.append(pltpu.make_async_copy(rrhs_h, rrhs, in_sem.at[7]))
    for ld in loads:
        ld.start()
    lax.fori_loop(1, Q, greet_plane, 0)
    lax.fori_loop(1, Z, greet_z, 0)

    def send(src, dst, sem_s, sem_r, dev):
        pltpu.make_async_remote_copy(
            src_ref=src, dst_ref=dst, send_sem=sem_s, recv_sem=sem_r, device_id=dev, device_id_type=MESH
        ).start()

    def arrive(view, sem):
        pltpu.make_async_copy(view, view, sem).wait()

    pending = []

    def sent(view, sem):
        pending.append((view, sem))

    def cols(h):
        return pl.ds(h * W, W)

    def tiled(n, fn, tile=TILE):
        def step(i, carry):
            fn(pl.multiple_of(i * tile, tile))
            return carry

        lax.fori_loop(0, n // tile, step, 0)

    def mask_child():
        @pl.when(c * CC + CC > r * CR)
        def _():
            def step(p, carry):
                piece = (p % Y) * CORES + p // Y
                rows = r * CR + piece * pc + lax.broadcasted_iota(jnp.int32, (pc, CC), 0)
                colid = c * CC + lax.broadcasted_iota(jnp.int32, (pc, CC), 1)
                blk = inv[p].astype(F32)
                blk = jnp.where(colid < rows, blk, jnp.where(colid == rows, 1.0, 0.0))
                inv[p] = blk.astype(BF)
                return carry

            lax.fori_loop(0, C, step, 0)

    def mask_root():
        for kk in range(2):
            loads[5 + kk].wait()

        @pl.when(me * RB + RB > r * RR)
        def _():
            def step(p, carry):
                g = p % G
                piece = (g // Y) * C + (g % Y) * CORES + p // G
                rows = r * RR + piece * pr + lax.broadcasted_iota(jnp.int32, (pr, RB), 0)
                colid = me * RB + lax.broadcasted_iota(jnp.int32, (pr, RB), 1)
                blk = root[p].astype(F32)
                blk = jnp.where(colid < rows, blk, jnp.where(colid == rows, 1.0, 0.0))
                root[p] = blk.astype(BF)
                return carry

            lax.fori_loop(0, 2 * G, step, 0)

    def make_ident():
        a = lax.broadcasted_iota(jnp.int32, (TILE, TILE), 0)
        b = lax.broadcasted_iota(jnp.int32, (TILE, TILE), 1)
        ident[...] = jnp.where(a == b, 1.0, 0.0).astype(BF)

    def transpose_into(x, xt, m, n, per):
        mt = min(512, m)
        for j in range(n // TILE):

            def step(i, carry):
                blk = x[pl.ds(i * (mt // per), mt // per), :, pl.ds(j * TILE, TILE)].reshape(mt, TILE)
                xt[pl.ds(j * TILE, TILE), pl.ds(pl.multiple_of(i * mt, mt), mt)] = nt(ident[...], blk).astype(BF)
                return carry

            lax.fori_loop(0, m // mt, step, 0)

    def make_slots():
        a = lax.broadcasted_iota(jnp.int32, (128, 128), 0)
        b = lax.broadcasted_iota(jnp.int32, (128, 128), 1)
        tri = jnp.where(a <= b, 1.0, 0.0).astype(BF)
        own_id = lax.broadcasted_iota(jnp.int32, (Q, 128), 0)
        base = jnp.zeros((Q, 1), F32)
        for i in range(U // 128):
            m = jnp.broadcast_to(cmap[:, i * 128 : (i + 1) * 128], (Q, 128))
            owner = m // RB
            hot = jnp.where(owner == own_id, 1.0, 0.0)
            count = nn(hot.astype(BF), tri)
            rank = jnp.sum(hot * (count + base - 1.0), axis=0, keepdims=True)
            base = base + jnp.sum(hot, axis=1, keepdims=True)
            slot[:, i * 128 : (i + 1) * 128] = jnp.broadcast_to(
                owner[0:8] * CAP + rank.astype(jnp.int32), (8, 128)
            )

    def make_sel():
        off = cmap[...] % RB
        row = lax.broadcasted_iota(jnp.int32, (16, U), 0)
        offb = jnp.broadcast_to(off, (16, U))
        probe = jnp.where(row == 0, offb // 16, jnp.where(row == 1, offb % 16, 1))
        probe = jnp.where(row < 3, probe, 0).astype(F32).astype(BF)

        def step(i, carry):
            ids = i * TILE + lax.broadcasted_iota(jnp.int32, (TILE, U), 0)
            blk = jnp.where(ids == slot[0:1, :], 1.0, 0.0).astype(BF)
            sel[pl.ds(pl.multiple_of(i * TILE, TILE), TILE), :] = blk
            info = nt(probe, blk)
            val = jnp.where(info[2:3] > 0.5, info[0:1] * 16.0 + info[1:2], float(RB))
            for j in range(TILE // 128):
                msend[i * (TILE // 128) + j] = jnp.broadcast_to(val[:, j * 128 : (j + 1) * 128], (8, 128))
            return carry

        lax.fori_loop(0, NS // TILE, step, 0)

    def send_meta():
        def step(d, carry):
            q = (me + d) % Q
            send(msend.at[q // 2], mrecv.at[me], msem.at[0], msem.at[1], plane_id(q))
            return carry

        lax.fori_loop(1, Q, step, 0)
        sent(mrecv.at[pl.ds(0, Q - 1)], msem.at[0])
        mrecv[me] = msend[me // 2]

    def make_lst():
        for kk in range(2):
            loads[3 + kk].wait()

        def step(i, carry):
            at = pl.ds(pl.multiple_of(i * TILE, TILE), TILE)
            blk = sel[at, :]
            for j in range(CR // 512):
                part = low[pl.ds(j * (512 // pc), 512 // pc)].reshape(512, U)
                lst[at, j * 512 : (j + 1) * 512] = nt(blk, part).astype(BF)
            return carry

        lax.fori_loop(0, NS // TILE, step, 0)

    def make_ls():
        def step(i, carry):
            part = low[pl.ds(i * (TILE // pc), TILE // pc)].reshape(TILE, U)
            at = pl.ds(pl.multiple_of(i * TILE, TILE), TILE)
            for j in range(NS // 512):
                ls[at, j * 512 : (j + 1) * 512] = nt(part, sel[j * 512 : (j + 1) * 512, :]).astype(BF)
            return carry

        lax.fori_loop(0, CR // TILE, step, 0)

    def make_asm():
        arrive(mrecv.at[pl.ds(0, Q - 1)], msem.at[1])

        def step(j, carry):
            lane = lax.broadcasted_iota(jnp.int32, (8, 128), 1)
            a, b = mrecv[2 * j], mrecv[2 * j + 1]
            ar, br = pltpu.roll(a, 64, 1), pltpu.roll(b, 64, 1)
            first = jnp.where(lane < 64, a, br)
            second = jnp.where(lane < 64, ar, b)
            kf = k.astype(F32)
            val = first * (1.0 - kf) + second * kf
            ids = lax.broadcasted_iota(jnp.int32, (RB, 128), 0).astype(F32)
            blk = jnp.where(ids == val[0:1, :], 1.0, 0.0).astype(BF)
            asm[:, pl.ds(pl.multiple_of(j * 128, 128), 128)] = blk
            return carry

        lax.fori_loop(0, Q // 2, step, 0)

    def make_asmt():
        def step(i, carry):
            at = pl.multiple_of(i * TILE, TILE)
            asmt[pl.ds(at, TILE), :] = nt(ident[...], asm[:, pl.ds(at, TILE)]).astype(BF)
            return carry

        lax.fori_loop(0, NS // TILE, step, 0)

    def coefficients(dref, oref, pref, fa, fb, start, n):
        first = (start // 128) * 128
        lane = lax.broadcasted_iota(jnp.int32, (128, 128), 1)
        even = lane % 2 == 0
        for i in range(max(1, n // 128)):
            at = pl.ds(pl.multiple_of(first + i * 128, 128), 128)
            a = jnp.broadcast_to(dref[:, at], (128, 128))
            o = jnp.broadcast_to(oref[:, at], (128, 128))
            p = jnp.broadcast_to(pref[:, at], (128, 128))
            partner = jnp.where(even, pltpu.roll(a, 127, 1), pltpu.roll(a, 1, 1))
            coup = jnp.where(p == 1, o, 0.0)
            coup = jnp.where(even, coup, pltpu.roll(coup, 1, 1))
            det = a * partner - coup * coup
            fa[pl.ds(i * 128, 128), :] = (partner / det).T
            fb[pl.ds(i * 128, 128), :] = (-coup / det).T

    def pivot(v, fa, fb, start, n):
        at = pl.ds(0, n) if n >= 128 else pl.ds(pl.multiple_of(start % 128, n), n)
        a = jnp.concatenate([fa[at, :]] * (W // 128), axis=1)
        b = jnp.concatenate([fb[at, :]] * (W // 128), axis=1)
        even = lax.broadcasted_iota(jnp.int32, (n, W), 0) % 2 == 0
        partner = jnp.where(even, pltpu.roll(v, n - 1, 0), pltpu.roll(v, 1, 0))
        return a * v + b * partner

    def make_coefs():
        coefficients(cdiag, coff, cpat, cfa, cfb, c * pc, pc)
        coefficients(rdiag, roff, rpat, rfa, rfb, me * pr, pr)

    half = CR // 2

    def col_core_send(h, s_a, r_a, st):
        send(s_a.at[h, pl.ds((1 - k) * half, half)], r_a.at[h], snd.at[h, st], rcv.at[h, st], sib)
        sent(r_a.at[h], snd.at[h, st])

    def col_y_send(h, s_a, r_a, s_b, r_b, st):
        arrive(r_a.at[h], rcv.at[h, st])
        s_b[h] = (s_a[h, pl.ds(pl.multiple_of(k * half, half), half), :].astype(F32) + r_a[h].astype(F32)).astype(BF)
        for d in range(1, Y):
            p = (y + d) % Y
            send(s_b.at[h, pl.ds(p * pc, pc)], r_b.at[h, pl.ds((d - 1) * pc, pc)], snd.at[h, st + 1], rcv.at[h, st + 1], y_id(d))
        sent(r_b.at[h], snd.at[h, st + 1])

    def col_sum(h, s_b, r_b, st):
        arrive(r_b.at[h], rcv.at[h, st + 1])
        acc = s_b[h, pl.ds(pl.multiple_of(y * pc, pc), pc), :].astype(F32)
        for d in range(Y - 1):
            acc = acc + r_b[h, d * pc : (d + 1) * pc, :].astype(F32)
        return acc

    def col_gather(h, buf, value, st, ys):
        at = pl.ds(pl.multiple_of(k * half + y * pc, pc), pc)
        buf[h, at, :] = value
        for d in range(1, Y):
            send(buf.at[h, at], buf.at[h, at], snd.at[h, st], ysem.at[h, ys, d - 1], y_id(d))
        send(buf.at[h, at], buf.at[h, at], snd.at[h, st + 1], rcv.at[h, st + 1], sib)
        sent(buf.at[h, pl.ds(0, (Y - 1) * pc)], snd.at[h, st])
        sent(buf.at[h, pl.ds(0, half)], snd.at[h, st + 1])

    def col_forward(h, buf, st, ys):
        for d in (1, Y - 1, 2) if Y == 4 else range(1, Y):
            at = pl.ds(pl.multiple_of(k * half + ((y + Y - d) % Y) * pc, pc), pc)
            arrive(buf.at[h, at], ysem.at[h, ys, d - 1])
            send(buf.at[h, at], buf.at[h, at], snd.at[h, st + 1], rcv.at[h, st + 1], sib)

    def col_gathered(h, buf, st):
        arrive(buf.at[h, pl.ds(0, half)], rcv.at[h, st + 1])

    def z_scatter(h, s, rr, n, st):
        def step(d, carry):
            to = (r + d) % Z
            send(s.at[h, pl.ds(to * n, n)], rr.at[h, pl.ds((d - 1) * n, n)], snd.at[h, st], rcv.at[h, st], z_id(d))
            return carry

        lax.fori_loop(1, Z, step, 0)
        sent(rr.at[h], snd.at[h, st])

    def z_sum(h, s, rr, n, st):
        arrive(rr.at[h], rcv.at[h, st])
        acc = s[h, pl.ds(pl.multiple_of(r * n, n), n), :].astype(F32)
        for d in range(Z - 1):
            acc = acc + rr[h, d * n : (d + 1) * n, :].astype(F32)
        return acc

    def z_gather(h, buf, value, n, st):
        at = pl.ds(pl.multiple_of(r * n, n), n)
        buf[h, at, :] = value

        def step(d, carry):
            send(buf.at[h, at], buf.at[h, at], snd.at[h, st], rcv.at[h, st], z_id(d))
            return carry

        lax.fori_loop(1, Z, step, 0)
        sent(buf.at[h, pl.ds(0, (Z - 1) * n)], snd.at[h, st])

    def z_gathered(h, buf, n, st):
        arrive(buf.at[h, pl.ds(0, (Z - 1) * n)], rcv.at[h, st])

    def exchange(h, mat, vec, s, rr, st):
        per = TILE // CAP
        groups = NS // TILE

        def step(i, carry):
            g = (me // per + 1 + i) % groups
            at = pl.multiple_of(g * TILE, TILE)
            s[h, pl.ds(at, TILE), :] = nn(mat[pl.ds(at, TILE), :], vec[h]).astype(BF)
            for j in range(per):
                q = g * per + j

                @pl.when(q != me)
                def _():
                    send(s.at[h, pl.ds(q * CAP, CAP)], rr.at[h, pl.ds(me * CAP, CAP)], snd.at[h, st], rcv.at[h, st], plane_id(q))

            return carry

        lax.fori_loop(0, groups, step, 0)
        sent(rr.at[h, pl.ds(0, NS - CAP)], snd.at[h, st])
        at = pl.ds(pl.multiple_of(me * CAP, CAP), CAP)
        rr[h, at, :] = s[h, at, :]

    def exchanged(h, rr, st):
        arrive(rr.at[h, pl.ds(0, NS - CAP)], rcv.at[h, st])

    def live(h):
        rows = r * CR + c * pc + lax.broadcasted_iota(jnp.int32, (pc, W), 0)
        return rows < piv[0]

    def a1(h):
        def fn(i):
            p = i // pc
            tile = inv[pl.ds(p, TILE // pc)].reshape(TILE, CC)
            s1[h, pl.ds(i, TILE), :] = nn(tile, rhs[:, h * W : (h + 1) * W]).astype(BF)

        tiled(CR, fn)

    def a2(h):
        col_core_send(h, s1, r1, 0)

    def b(h):
        col_y_send(h, s1, r1, s2, r2, 0)

    def cc(h):
        acc = col_sum(h, s2, r2, 0)
        solved = jnp.where(live(h), acc, 0.0).astype(BF)
        col_gather(h, sol, solved, 2, 0)
        scaled[h] = pivot(solved.astype(F32), cfa, cfb, c * pc, pc)

    def d(h):
        col_forward(h, sol, 2, 0)

    def e(h):
        col_gathered(h, sol, 2)
        exchange(h, lst, sol, s3, r3, 4)

    def f(h):
        exchanged(h, r3, 4)

        def fn(i):
            s4[h, pl.ds(i, TILE), :] = nn(asm[pl.ds(i, TILE), :], r3[h]).astype(BF)

        tiled(RB, fn)
        z_scatter(h, s4, r4, pz, 5)

    def g(h):
        acc = z_sum(h, s4, r4, pz, 5)
        mine = rrhs[pl.ds(pl.multiple_of(r * pz, pz), pz), h * W : (h + 1) * W].astype(F32)
        z_gather(h, upd, (mine - acc).astype(BF), pz, 6)

    def hh(h):
        z_gathered(h, upd, pz, 6)

        def fn(i):
            tile = root[pl.ds(i // pr, TILE // pr)].reshape(TILE, RB)
            s6[h, pl.ds(i, TILE), :] = nn(tile, upd[h]).astype(BF)

        tiled(RR, fn)
        rh = RR // 2
        send(s6.at[h, pl.ds((1 - k) * rh, rh)], r6.at[h], snd.at[h, 7], rcv.at[h, 7], sib)
        sent(r6.at[h], snd.at[h, 7])

    def i_(h):
        arrive(r6.at[h], rcv.at[h, 7])
        rh = RR // 2
        gi = t * Y + y

        def step(j, carry):
            p = (gi + 1 + j) % G
            at = pl.ds(pl.multiple_of(p * pr, pr), pr)
            mine = pl.ds(pl.multiple_of(k * rh + p * pr, pr), pr)
            s6b[h, at, :] = (s6[h, mine, :].astype(F32) + r6[h, at, :].astype(F32)).astype(BF)

            @pl.when(p != gi)
            def _():
                send(s6b.at[h, at], r6b.at[h, pl.ds(j * pr, pr)], snd.at[h, 8], rcv.at[h, 8], g_id(p))

            return carry

        lax.fori_loop(0, G, step, 0)
        sent(r6b.at[h], snd.at[h, 8])

    def j_(h):
        arrive(r6b.at[h], rcv.at[h, 8])
        gi = t * Y + y
        acc = s6b[h, pl.ds(pl.multiple_of(gi * pr, pr), pr), :].astype(F32)
        for n in range(G - 1):
            acc = acc + r6b[h, n * pr : (n + 1) * pr, :].astype(F32)
        value = pivot(acc, rfa, rfb, me * pr, pr).astype(BF)
        at = pl.ds(pl.multiple_of((k * G + gi) * pr, pr), pr)
        rsc[h, at, :] = value

        def step(n, carry):
            send(rsc.at[h, at], rsc.at[h, at], snd.at[h, 9], rcv.at[h, 9], g_id((gi + n) % G))
            return carry

        lax.fori_loop(1, G, step, 0)
        sent(rsc.at[h, pl.ds(0, (G - 1) * pr)], snd.at[h, 9])

    def k_(h):
        rh = RR // 2
        arrive(rsc.at[h, pl.ds(0, (G - 1) * pr)], rcv.at[h, 9])
        mine = pl.ds(k * rh, rh)
        send(rsc.at[h, mine], rsc.at[h, mine], snd.at[h, 10], rcv.at[h, 10], sib)
        sent(rsc.at[h, pl.ds(0, rh)], snd.at[h, 10])

    def l_(h):
        arrive(rsc.at[h, pl.ds(0, RR // 2)], rcv.at[h, 10])

        def fn(i):
            s8[h, pl.ds(i, TILE), :] = nn(roott[pl.ds(i, TILE), :], rsc[h]).astype(BF)

        tiled(RB, fn)
        z_scatter(h, s8, r8, pz, 11)

    def m_(h):
        z_gather(h, rs, z_sum(h, s8, r8, pz, 11).astype(BF), pz, 12)

    def n_(h):
        z_gathered(h, rs, pz, 12)
        exchange(h, asmt, rs, s10, r10, 13)
        out_r[:, h * W : (h + 1) * W] = rs[h]

    def o_(h):
        exchanged(h, r10, 13)

        def fn(i):
            s11[h, pl.ds(i, TILE), :] = nn(ls[pl.ds(i, TILE), :], r10[h]).astype(BF)

        tiled(CR, fn)
        col_core_send(h, s11, r11, 14)

    def p_(h):
        col_y_send(h, s11, r11, s11b, r11b, 14)

    def q_(h):
        acc = col_sum(h, s11b, r11b, 14)
        value = jnp.where(live(h), scaled[h] - acc, 0.0).astype(BF)
        col_gather(h, res, value, 16, 1)

    def r_(h):
        col_forward(h, res, 16, 1)

    def s_(h):
        col_gathered(h, res, 16)

        def fn(i):
            s13[h, pl.ds(i, TILE), :] = nn(invt[pl.ds(i, TILE), :], res[h]).astype(BF)

        tiled(CC, fn)
        z_scatter(h, s13, r13, pu, 18)

    def t_(h):
        z_gather(h, cs, z_sum(h, s13, r13, pu, 18).astype(BF), pu, 19)

    def u_(h):
        z_gathered(h, cs, pu, 19)
        out_c[:, h * W : (h + 1) * W] = cs[h]

    for n in range(3):
        loads[n].wait()
    mask_child()
    for h in range(H):
        a1(h)
    pl.semaphore_wait(barrier, Q - 1 + Z - 1)
    plan = [
        (a2, [make_slots, make_sel]),
        (b, [send_meta, make_coefs, make_lst]),
        (cc, [make_ident]),
        (d, []),
        (e, [make_asm, mask_root]),
        (f, [make_ls]),
        (g, [lambda: transpose_into(root, roott, RR, RB, pr)]),
        (hh, []),
        (i_, [make_asmt]),
        (j_, [lambda: transpose_into(inv, invt, CR, CC, pc)]),
        (k_, []), (l_, []), (m_, []), (n_, []), (o_, []), (p_, []), (q_, []), (r_, []), (s_, []), (t_, []), (u_, []),
    ]
    for stage, background in plan:
        if stage is g:
            loads[7].wait()
        for h in range(H):
            stage(h)
        for work in background:
            work()
    for view, sem in pending:
        arrive(view, sem)


def shards(dims, *args):
    (child_inverse, child_lower, child_rhs, child_diag, child_off, child_pattern, child_pivots, child_map,
     root_inverse, root_rhs, root_diag, root_off, root_pattern) = args
    T, Z, Y, CR, CC, U, RB, RR, R, H = dims
    C, Q, G, W = Y * CORES, T * Y * CORES, T * Y, R // H
    NS = Q * CAP
    pc, pr, pz, pu = CR // C, RR // Q, RB // Z, CC // Z

    def chain(rows):
        return pltpu.VMEM((H, rows, W), BF)

    vm = lambda *shape: pltpu.VMEM(shape, BF)
    fm = lambda *shape: pltpu.VMEM(shape, F32)
    half = CR // 2
    scratch = [
        vm(C, pc, CC), vm(CC, CR), vm(C, pc, U), vm(NS, CR), vm(CR, NS), vm(NS, U), vm(Q, pr, RB), vm(RB, RR),
        vm(RB, NS), vm(NS, RB), vm(TILE, TILE), vm(CC, R), vm(RB, R),
        pltpu.VMEM((8, U), jnp.int32), fm(Q // 2, 8, 128), fm(Q, 8, 128),
        fm(max(pc, 128), 128), fm(max(pc, 128), 128), fm(max(pr, 128), 128), fm(max(pr, 128), 128), fm(H, pc, W),
        chain(CR), chain(half), chain(half), chain((Y - 1) * pc), chain(CR), chain(NS), chain(NS), chain(RB),
        chain((Z - 1) * pz), chain(RB),
        chain(RR), chain(RR // 2), chain(RR // 2), chain((G - 1) * pr), chain(RR), chain(RB), chain((Z - 1) * pz),
        chain(RB), chain(NS), chain(NS),
        chain(CR), chain(half), chain(half), chain((Y - 1) * pc), chain(CR), chain(CC), chain((Z - 1) * pu), chain(CC),
        pltpu.SemaphoreType.DMA((8,)), pltpu.SemaphoreType.DMA((H, 20)), pltpu.SemaphoreType.DMA((H, 20)),
        pltpu.SemaphoreType.DMA((H, 2, Y - 1)), pltpu.SemaphoreType.DMA((2,)),
    ]
    anyspec = pl.BlockSpec(memory_space=pl.ANY)
    vspec = pl.BlockSpec(memory_space=pltpu.VMEM)
    flops = 2 * R * (2 * CR * CC + 2 * NS * CR + 2 * RB * NS + 2 * RR * RB)
    child, rooted = pl.pallas_call(
        functools.partial(body, dims),
        name="substitution",
        out_shape=(jax.ShapeDtypeStruct((CC, R), BF), jax.ShapeDtypeStruct((RB, R), BF)),
        in_specs=[anyspec] * 5 + [vspec] * 7 + [pl.BlockSpec(memory_space=pltpu.SMEM)],
        out_specs=(vspec, vspec),
        scratch_shapes=scratch,
        cost_estimate=pl.CostEstimate(flops=flops, bytes_accessed=8 << 20, transcendentals=0),
        compiler_params=pltpu.CompilerParams(collective_id=0, has_side_effects=True, vmem_limit_bytes=58 << 20),
    )(
        child_inverse.reshape(Y, CORES, pc, CC),
        child_lower.reshape(Y, CORES, pc, U),
        root_inverse.reshape(G, CORES, pr, RB),
        child_rhs.reshape(CC, R),
        root_rhs,
        child_diag.reshape(1, CR),
        child_off.reshape(1, CR),
        child_pattern.reshape(1, CR),
        root_diag.reshape(1, RR),
        root_off.reshape(1, RR),
        root_pattern.reshape(1, RR),
        child_map.reshape(1, U),
        child_pivots,
    )
    return (child.astype(F32)[None], rooted.astype(F32))


def solution(mesh):
    T, Z, C = mesh.shape["team"], mesh.shape["row"], mesh.shape["col"]

    def run(*args):
        pc_, uc = args[0].shape[1], args[1].shape[2]
        fr, R = args[9].shape
        dims = (T, Z, C // CORES, pc_ // Z, pc_ // C, uc // C, fr // (T * C), fr // Z, R, CHAINS)
        return jax.shard_map(
            functools.partial(shards, dims),
            mesh=mesh,
            in_specs=(
                P("team", "row", "col"),
                P("team", "row", "col"),
                P("team", "col", None),
                P("team", "row"),
                P("team", "row"),
                P("team", "row"),
                P("team"),
                P("team", "col"),
                P("row", ("team", "col")),
                P(("team", "col"), None),
                P("row"),
                P("row"),
                P("row"),
            ),
            out_specs=(P("team", "col", None), P(("team", "col"), None)),
            check_vma=False,
        )(*args)

    return run
```

```python
import functools

import jax
import jax.numpy as jnp
from jax import lax
from jax.experimental import pallas as pl
from jax.experimental.pallas import tpu as pltpu
from jax.sharding import PartitionSpec as P

BF = jnp.bfloat16
F32 = jnp.float32
MESH = pl.DeviceIdType.MESH
CORES = 2
CAP = 64
TILE = 256
MT = 512
XT = 256
UNROLL = False
CHAINS = 2
ORDER = ["a0", "a1", "sel", "b0", "b1", "meta", "lst0", "c0", "c1", "ident", "lst1", "d0", "d1", "e0", "e1"]
ORDER += ["asm", "f0", "rrhs", "mask", "coefs", "f1", "roott", "g0", "g1", "h0", "i0", "h1", "i1", "j0", "asmt"]
ORDER += ["j1", "k0", "l0", "k1", "l1", "ls0", "m0", "ls1", "m1", "n0", "n1", "invt", "o0", "p0", "o1", "q0", "p1"]
ORDER += ["r0", "q1", "s0", "r1", "s1", "S0", "S1", "t0", "t1", "T0", "T1", "u0", "u1"]
TREE = True
RST = False
OUT = pltpu.VMEM


def nn(a, b):
    return jnp.dot(a, b, preferred_element_type=F32)


def nt(a, b):
    return lax.dot_general(a, b, (((1,), (1,)), ((), ())), preferred_element_type=F32)


def body(dims, *refs):
    T, Z, Y, CR, CC, U, RB, RR, R, H = dims
    C = Y * CORES
    Q = T * C
    G = T * Y
    W = R // H
    NS = Q * CAP
    pc, pr, pz, pu = CR // C, RR // Q, RB // Z, CC // Z
    it = iter(refs)
    take = lambda n: [next(it) for _ in range(n)]
    inv_h, low_h, root_h, rhs_h, rrhs_h = take(5)
    small_h = take(8)
    out_c, out_r = take(2)
    inv, invt, low, lst, ls, sel, root, roott, asm, asmt, ident, rhs, rrhs = take(13)
    slot, msend, mrecv, cfa, cfb, rfa, rfb, scaled = take(8)
    s1, r1, s2, r2, sol, s3, r3, s4, r4, upd = take(10)
    s6, r6, s6b, r6b, rsc, s8, r8, rs, s10, r10 = take(10)
    s11, r11, s11b, r11b, res, s13, r13, mid, cs = take(9)
    small = take(8)
    cdiag, coff, cpat, rdiag, roff, rpat, cmap, piv = small
    in_sem, small_sem, snd, rcv, ysem, zsem, msem = take(7)

    t = lax.axis_index("team")
    r = lax.axis_index("row")
    c = lax.axis_index("col")
    y = c // CORES
    k = c % CORES
    me = t * C + c
    sib = (t, r, y * CORES + (1 - k))

    def plane_id(q):
        return (t * 0 + q // C, r, q % C)

    def z_id(d):
        return (t, (r + d) % Z, c)

    def y_id(d):
        return (t, r, ((y + d) % Y) * CORES + k)

    def g_id(g):
        return (g // Y, r, (g % Y) * CORES + k)

    barrier = pltpu.get_barrier_semaphore()

    def greet_plane(d, carry):
        pl.semaphore_signal(barrier, inc=1, device_id=plane_id((me + d) % Q), device_id_type=MESH)
        return carry

    def greet_z(d, carry):
        pl.semaphore_signal(barrier, inc=1, device_id=z_id(d), device_id_type=MESH)
        return carry

    loads = [pltpu.make_async_copy(rhs_h, rhs, in_sem.at[0])]
    for kk in range(CORES):
        loads.append(pltpu.make_async_copy(inv_h.at[:, kk], inv.at[pl.ds(kk * Y, Y)], in_sem.at[1 + kk]))
    for kk in range(CORES):
        loads.append(pltpu.make_async_copy(low_h.at[:, kk], low.at[pl.ds(kk * Y, Y)], in_sem.at[3 + kk]))
    for kk in range(CORES):
        loads.append(pltpu.make_async_copy(root_h.at[:, kk], root.at[pl.ds(kk * G, G)], in_sem.at[5 + kk]))
    loads.append(pltpu.make_async_copy(rrhs_h, rrhs, in_sem.at[7]))
    small_loads = [pltpu.make_async_copy(a, b, small_sem.at[n]) for n, (a, b) in enumerate(zip(small_h, small))]
    small_loads[6].start()
    for ld in loads[:3]:
        ld.start()
    lax.fori_loop(1, Q, greet_plane, 0, unroll=UNROLL)
    lax.fori_loop(1, Z, greet_z, 0, unroll=UNROLL)
    for ld in small_loads[7:] + loads[3:] + small_loads[:6]:
        ld.start()

    def send(src, dst, sem_s, sem_r, dev):
        pltpu.make_async_remote_copy(
            src_ref=src, dst_ref=dst, send_sem=sem_s, recv_sem=sem_r, device_id=dev, device_id_type=MESH
        ).start()

    def arrive(view, sem):
        pltpu.make_async_copy(view, view, sem).wait()

    pending = []

    def sent(view, sem):
        pending.append((view, sem))

    def cols(h):
        return pl.ds(h * W, W)

    def halves(n, fn, push):
        def step(i, carry):
            fn(pl.multiple_of(((1 - k) * (n // 2 // MT) + i) % (n // MT) * MT, MT))

            @pl.when(i == n // 2 // MT - 1)
            def _():
                push()

            return carry

        lax.fori_loop(0, n // MT, step, 0)

    def tiled(n, fn, tile=MT):
        def step(i, carry):
            fn(pl.multiple_of(i * tile, tile))
            return carry

        lax.fori_loop(0, n // tile, step, 0)

    def mask_child():
        @pl.when(c > r)
        def _():
            def step(p, carry):
                inv[p] = jnp.zeros((pc, CC), BF)
                return carry

            lax.fori_loop(0, C, step, 0)

        @pl.when(c == r)
        def _():
            rows = lax.broadcasted_iota(jnp.int32, (pc, pc), 0)
            colid = lax.broadcasted_iota(jnp.int32, (pc, pc), 1)
            for p in range(C):
                at = ((p % Y) * CORES + p // Y) * pc
                blk = inv[p, :, at : at + pc].astype(F32)
                blk = jnp.where(colid < rows, blk, jnp.where(colid == rows, 1.0, 0.0))
                inv[p, :, at : at + pc] = blk.astype(BF)
                if at + pc < CC:
                    inv[p, :, at + pc :] = jnp.zeros((pc, CC - at - pc), BF)

    def mask_root():
        for kk in range(2):
            loads[5 + kk].wait()

        @pl.when(me * RB + RB > r * RR)
        def _():
            def step(p, carry):
                g = p % G
                piece = (g // Y) * C + (g % Y) * CORES + p // G
                rows = r * RR + piece * pr + lax.broadcasted_iota(jnp.int32, (pr, RB), 0)
                colid = me * RB + lax.broadcasted_iota(jnp.int32, (pr, RB), 1)
                blk = root[p].astype(F32)
                blk = jnp.where(colid < rows, blk, jnp.where(colid == rows, 1.0, 0.0))
                root[p] = blk.astype(BF)
                return carry

            lax.fori_loop(0, 2 * G, step, 0)

    def make_ident():
        a = lax.broadcasted_iota(jnp.int32, (TILE, TILE), 0)
        b = lax.broadcasted_iota(jnp.int32, (TILE, TILE), 1)
        ident[...] = jnp.where(a == b, 1.0, 0.0).astype(BF)

    def transpose_into(x, xt, m, n, per):
        mt = min(512, m)
        for j in range(n // TILE):

            def step(i, carry):
                blk = x[pl.ds(i * (mt // per), mt // per), :, pl.ds(j * TILE, TILE)].reshape(mt, TILE)
                xt[pl.ds(j * TILE, TILE), pl.ds(pl.multiple_of(i * mt, mt), mt)] = nt(ident[...], blk).astype(BF)
                return carry

            lax.fori_loop(0, m // mt, step, 0)

    def make_slots():
        a = lax.broadcasted_iota(jnp.int32, (128, 128), 0)
        b = lax.broadcasted_iota(jnp.int32, (128, 128), 1)
        tri = jnp.where(a <= b, 1.0, 0.0).astype(BF)
        own_id = lax.broadcasted_iota(jnp.int32, (Q, 128), 0)
        base = jnp.zeros((Q, 1), F32)
        for i in range(U // 128):
            m = jnp.broadcast_to(cmap[:, i * 128 : (i + 1) * 128], (Q, 128))
            owner = m // RB
            hot = jnp.where(owner == own_id, 1.0, 0.0)
            count = nn(hot.astype(BF), tri)
            rank = jnp.sum(hot * (count + base - 1.0), axis=0, keepdims=True)
            base = base + jnp.sum(hot, axis=1, keepdims=True)
            slot[:, i * 128 : (i + 1) * 128] = jnp.broadcast_to(
                owner[0:8] * CAP + rank.astype(jnp.int32), (8, 128)
            )

    def make_sel():
        off = cmap[...] % RB
        row = lax.broadcasted_iota(jnp.int32, (16, U), 0)
        offb = jnp.broadcast_to(off, (16, U))
        probe = jnp.where(row == 0, offb // 16, jnp.where(row == 1, offb % 16, 1))
        probe = jnp.where(row < 3, probe, 0).astype(F32).astype(BF)

        def step(i, carry):
            ids = i * TILE + lax.broadcasted_iota(jnp.int32, (TILE, U), 0)
            blk = jnp.where(ids == slot[0:1, :], 1.0, 0.0).astype(BF)
            sel[pl.ds(pl.multiple_of(i * TILE, TILE), TILE), :] = blk
            info = nt(probe, blk)
            val = jnp.where(info[2:3] > 0.5, info[0:1] * 16.0 + info[1:2], float(RB))
            for j in range(TILE // 128):
                msend[i * (TILE // 128) + j] = jnp.broadcast_to(val[:, j * 128 : (j + 1) * 128], (8, 128))
            return carry

        lax.fori_loop(0, NS // TILE, step, 0)

    def send_meta():
        def step(d, carry):
            q = (me + d) % Q
            send(msend.at[q // 2], mrecv.at[me], msem.at[0], msem.at[1], plane_id(q))
            return carry

        lax.fori_loop(1, Q, step, 0)
        sent(mrecv.at[pl.ds(0, Q - 1)], msem.at[0])
        mrecv[me] = msend[me // 2]

    def make_lst(part_no):
        if part_no == 0:
            for kk in range(2):
                loads[3 + kk].wait()

        def step(i, carry):
            at = pl.ds(pl.multiple_of(i * TILE, TILE), TILE)
            blk = sel[at, :]
            for j in range(CR // 512):
                part = low[pl.ds(j * (512 // pc), 512 // pc)].reshape(512, U)
                lst[at, j * 512 : (j + 1) * 512] = nt(blk, part).astype(BF)
            return carry

        count = NS // TILE // 2
        lax.fori_loop(part_no * count, (part_no + 1) * count, step, 0)

    def make_ls(part_no):
        def step(i, carry):
            part = low[pl.ds(i * (TILE // pc), TILE // pc)].reshape(TILE, U)
            at = pl.ds(pl.multiple_of(i * TILE, TILE), TILE)
            for j in range(NS // 512):
                ls[at, j * 512 : (j + 1) * 512] = nt(part, sel[j * 512 : (j + 1) * 512, :]).astype(BF)
            return carry

        count = CR // TILE // 2
        lax.fori_loop(part_no * count, (part_no + 1) * count, step, 0)

    def make_asm():
        arrive(mrecv.at[pl.ds(0, Q - 1)], msem.at[1])

        def step(j, carry):
            lane = lax.broadcasted_iota(jnp.int32, (8, 128), 1)
            a, b = mrecv[2 * j], mrecv[2 * j + 1]
            ar, br = pltpu.roll(a, 64, 1), pltpu.roll(b, 64, 1)
            first = jnp.where(lane < 64, a, br)
            second = jnp.where(lane < 64, ar, b)
            kf = k.astype(F32)
            val = first * (1.0 - kf) + second * kf
            ids = lax.broadcasted_iota(jnp.int32, (RB, 128), 0).astype(F32)
            blk = jnp.where(ids == val[0:1, :], 1.0, 0.0).astype(BF)
            asm[:, pl.ds(pl.multiple_of(j * 128, 128), 128)] = blk
            return carry

        lax.fori_loop(0, Q // 2, step, 0)

    def make_asmt():
        def step(i, carry):
            at = pl.multiple_of(i * TILE, TILE)
            asmt[pl.ds(at, TILE), :] = nt(ident[...], asm[:, pl.ds(at, TILE)]).astype(BF)
            return carry

        lax.fori_loop(0, NS // TILE, step, 0)

    def coefficients(dref, oref, pref, fa, fb, start, n):
        first = (start // 128) * 128
        lane = lax.broadcasted_iota(jnp.int32, (128, 128), 1)
        even = lane % 2 == 0
        for i in range(max(1, n // 128)):
            at = pl.ds(pl.multiple_of(first + i * 128, 128), 128)
            a = jnp.broadcast_to(dref[:, at], (128, 128))
            o = jnp.broadcast_to(oref[:, at], (128, 128))
            p = jnp.broadcast_to(pref[:, at], (128, 128))
            partner = jnp.where(even, pltpu.roll(a, 127, 1), pltpu.roll(a, 1, 1))
            coup = jnp.where(p == 1, o, 0.0)
            coup = jnp.where(even, coup, pltpu.roll(coup, 1, 1))
            det = a * partner - coup * coup
            fa[pl.ds(i * 128, 128), :] = (partner / det).T
            fb[pl.ds(i * 128, 128), :] = (-coup / det).T

    def pivot(v, fa, fb, start, n):
        at = pl.ds(0, n) if n >= 128 else pl.ds(pl.multiple_of(start % 128, n), n)
        a = jnp.concatenate([fa[at, :]] * (W // 128), axis=1)
        b = jnp.concatenate([fb[at, :]] * (W // 128), axis=1)
        even = lax.broadcasted_iota(jnp.int32, (n, W), 0) % 2 == 0
        partner = jnp.where(even, pltpu.roll(v, n - 1, 0), pltpu.roll(v, 1, 0))
        return a * v + b * partner

    def make_coefs():
        coefficients(cdiag, coff, cpat, cfa, cfb, c * pc, pc)
        coefficients(rdiag, roff, rpat, rfa, rfb, me * pr, pr)

    half = CR // 2

    def col_core_send(h, s_a, r_a, st):
        send(s_a.at[h, pl.ds((1 - k) * half, half)], r_a.at[h], snd.at[h, st], rcv.at[h, st], sib)

    def col_y_send(h, s_a, r_a, s_b, r_b, st):
        arrive(r_a.at[h], rcv.at[h, st])
        s_b[h] = (s_a[h, pl.ds(pl.multiple_of(k * half, half), half), :].astype(F32) + r_a[h].astype(F32)).astype(BF)
        for d in range(1, Y):
            p = (y + d) % Y
            send(s_b.at[h, pl.ds(p * pc, pc)], r_b.at[h, pl.ds((d - 1) * pc, pc)], snd.at[h, st + 1], rcv.at[h, st + 1], y_id(d))
        sent(r_b.at[h], snd.at[h, st + 1])

    def col_sum(h, s_b, r_b, st):
        arrive(r_b.at[h], rcv.at[h, st + 1])
        acc = s_b[h, pl.ds(pl.multiple_of(y * pc, pc), pc), :].astype(F32)
        for d in range(Y - 1):
            acc = acc + r_b[h, d * pc : (d + 1) * pc, :].astype(F32)
        return acc

    def col_gather(h, buf, value, st, ys):
        at = pl.ds(pl.multiple_of(k * half + y * pc, pc), pc)
        buf[h, at, :] = value
        for d in range(1, Y):
            send(buf.at[h, at], buf.at[h, at], snd.at[h, st], ysem.at[h, ys, d - 1], y_id(d))
        send(buf.at[h, at], buf.at[h, at], snd.at[h, st + 1], rcv.at[h, st + 1], sib)
        sent(buf.at[h, pl.ds(0, (Y - 1) * pc)], snd.at[h, st])
        sent(buf.at[h, pl.ds(0, half)], snd.at[h, st + 1])

    def col_forward(h, buf, st, ys):
        for d in (1, Y - 1, 2) if Y == 4 else range(1, Y):
            at = pl.ds(pl.multiple_of(k * half + ((y + Y - d) % Y) * pc, pc), pc)
            arrive(buf.at[h, at], ysem.at[h, ys, d - 1])
            send(buf.at[h, at], buf.at[h, at], snd.at[h, st + 1], rcv.at[h, st + 1], sib)

    def col_gathered(h, buf, st):
        arrive(buf.at[h, pl.ds(0, half)], rcv.at[h, st + 1])

    def far(i):
        return Z // 2 + (1 - 2 * (i % 2)) * ((i + 1) // 2)

    def z_scatter(h, s, rr, n, st):
        def step(i, carry):
            d = far(i)
            to = (r + d) % Z
            send(s.at[h, pl.ds(to * n, n)], rr.at[h, pl.ds((d - 1) * n, n)], snd.at[h, st], rcv.at[h, st], z_id(d))
            return carry

        lax.fori_loop(0, Z - 1, step, 0, unroll=UNROLL)
        sent(rr.at[h], snd.at[h, st])

    def z_sum(h, s, rr, n, st):
        arrive(rr.at[h], rcv.at[h, st])
        acc = s[h, pl.ds(pl.multiple_of(r * n, n), n), :].astype(F32)
        for d in range(Z - 1):
            acc = acc + rr[h, d * n : (d + 1) * n, :].astype(F32)
        return acc

    def z_gather(h, buf, value, n, st):
        at = pl.ds(pl.multiple_of(r * n, n), n)
        buf[h, at, :] = value

        def step(i, carry):
            send(buf.at[h, at], buf.at[h, at], snd.at[h, st], rcv.at[h, st], z_id(far(i)))
            return carry

        lax.fori_loop(0, Z - 1, step, 0, unroll=UNROLL)
        sent(buf.at[h, pl.ds(0, (Z - 1) * n)], snd.at[h, st])

    def z_gathered(h, buf, n, st):
        arrive(buf.at[h, pl.ds(0, (Z - 1) * n)], rcv.at[h, st])

    def z_tree_scatter(h, s, mid, rr, n, st):
        def part(to):
            return s.at[h, pl.ds(((r + to) % Z) * n, n)]

        for i, (to, via) in enumerate(((3, 1), (Z - 3, Z - 1), (4, (2, Z - 2)[h % 2]))):
            sem = zsem.at[h, 2 + (i if i < 2 else h % 2)]
            send(part(to), mid.at[h, pl.ds(i * n, n)], snd.at[h, st], sem, z_id(via))
        for i, to in enumerate((1, Z - 1)):
            send(part(to), rr.at[h, pl.ds(i * n, n)], snd.at[h, st], rcv.at[h, st], z_id(to))
        sent(s.at[h, pl.ds(0, 5 * n)], snd.at[h, st])

    def z_tree_pass(h, s, mid, rr, n, st):
        for i, to in enumerate((2, Z - 2)):
            both = i == h % 2
            view = mid.at[h, pl.ds(0, (2 if both else 1) * n)]
            arrive(view, zsem.at[h, 2 + i])
            at = pl.ds(pl.multiple_of(((r + to) % Z) * n, n), n)
            acc = s[h, at, :].astype(F32) + mid[h, i * n : (i + 1) * n, :].astype(F32)
            if both:
                acc = acc + mid[h, 2 * n : 3 * n, :].astype(F32)
            s[h, at, :] = acc.astype(BF)
            send(s.at[h, at], rr.at[h, pl.ds((2 + i) * n, n)], snd.at[h, st + 1], rcv.at[h, st], z_id(to))
        sent(s.at[h, pl.ds(0, 2 * n)], snd.at[h, st + 1])

    def z_tree_sum(h, s, rr, n, st):
        arrive(rr.at[h, pl.ds(0, 4 * n)], rcv.at[h, st])
        acc = s[h, pl.ds(pl.multiple_of(r * n, n), n), :].astype(F32)
        for d in range(4):
            acc = acc + rr[h, d * n : (d + 1) * n, :].astype(F32)
        return acc

    def z_tree(h, buf, value, n, st):
        at = pl.ds(pl.multiple_of(r * n, n), n)
        buf[h, at, :] = value
        for i, d in enumerate((2, Z - 2)):
            send(buf.at[h, at], buf.at[h, at], snd.at[h, st], zsem.at[h, i], z_id(d))
        for d in (1, Z - 1):
            send(buf.at[h, at], buf.at[h, at], snd.at[h, st], rcv.at[h, st], z_id(d))
        sent(buf.at[h, pl.ds(0, (Z - 1) * n)], snd.at[h, st])

    def z_tree_forward(h, buf, n, st):
        for i, d in enumerate((2, Z - 2)):
            at = pl.ds(pl.multiple_of(((r + Z - d) % Z) * n, n), n)
            arrive(buf.at[h, at], zsem.at[h, i])
            if i == h % 2:
                send(buf.at[h, at], buf.at[h, at], snd.at[h, st], rcv.at[h, st], z_id(d))
            send(buf.at[h, at], buf.at[h, at], snd.at[h, st], rcv.at[h, st], z_id((1, Z - 1)[i]))

    def exchange(h, mat, vec, s, rr, st):
        per = XT // CAP
        groups = NS // XT

        def step(i, carry):
            g = (me // per + 1 + i) % groups
            at = pl.multiple_of(g * XT, XT)
            s[h, pl.ds(at, XT), :] = nn(mat[pl.ds(at, XT), :], vec[h]).astype(BF)
            for j in range(per):
                q = g * per + j

                @pl.when(q != me)
                def _():
                    send(s.at[h, pl.ds(q * CAP, CAP)], rr.at[h, pl.ds(me * CAP, CAP)], snd.at[h, st], rcv.at[h, st], plane_id(q))

            return carry

        lax.fori_loop(0, groups, step, 0)
        sent(rr.at[h, pl.ds(0, NS - CAP)], snd.at[h, st])
        at = pl.ds(pl.multiple_of(me * CAP, CAP), CAP)
        rr[h, at, :] = s[h, at, :]

    def exchanged(h, rr, st):
        arrive(rr.at[h, pl.ds(0, NS - CAP)], rcv.at[h, st])

    def live(h):
        rows = r * CR + c * pc + lax.broadcasted_iota(jnp.int32, (pc, W), 0)
        return rows < piv[...]

    def a1(h):
        def fn(i):
            p = i // pc
            tile = inv[pl.ds(p, MT // pc)].reshape(MT, CC)
            s1[h, pl.ds(i, MT), :] = nn(tile, rhs[:, h * W : (h + 1) * W]).astype(BF)

        return fn

    def b(h):
        col_y_send(h, s1, r1, s2, r2, 0)

    def cc(h):
        acc = col_sum(h, s2, r2, 0)
        solved = jnp.where(live(h), acc, 0.0).astype(BF)
        col_gather(h, sol, solved, 2, 0)

    def d(h):
        col_forward(h, sol, 2, 0)

    def e(h):
        col_gathered(h, sol, 2)
        exchange(h, lst, sol, s3, r3, 4)

    def f(h):
        exchanged(h, r3, 4)

        def fn(i):
            s4[h, pl.ds(i, MT), :] = nn(asm[pl.ds(i, MT), :], r3[h]).astype(BF)

        tiled(RB, fn)
        z_scatter(h, s4, r4, pz, 5)

    def g(h):
        acc = z_sum(h, s4, r4, pz, 5)
        mine = rrhs[pl.ds(pl.multiple_of(r * pz, pz), pz), h * W : (h + 1) * W].astype(F32)
        z_gather(h, upd, (mine - acc).astype(BF), pz, 6)

    def hh(h):
        z_gathered(h, upd, pz, 6)

        def fn(i):
            tile = root[pl.ds(i // pr, MT // pr)].reshape(MT, RB)
            s6[h, pl.ds(i, MT), :] = nn(tile, upd[h]).astype(BF)

        rh = RR // 2
        halves(RR, fn, lambda: send(s6.at[h, pl.ds((1 - k) * rh, rh)], r6.at[h], snd.at[h, 7], rcv.at[h, 7], sib))
        sent(r6.at[h], snd.at[h, 7])

    def i_(h):
        arrive(r6.at[h], rcv.at[h, 7])
        rh = RR // 2
        gi = t * Y + y

        def step(j, carry):
            p = (gi + 1 + j) % G
            at = pl.ds(pl.multiple_of(p * pr, pr), pr)
            mine = pl.ds(pl.multiple_of(k * rh + p * pr, pr), pr)
            s6b[h, at, :] = (s6[h, mine, :].astype(F32) + r6[h, at, :].astype(F32)).astype(BF)

            @pl.when(p != gi)
            def _():
                send(s6b.at[h, at], r6b.at[h, pl.ds(j * pr, pr)], snd.at[h, 8], rcv.at[h, 8], g_id(p))

            return carry

        lax.fori_loop(0, G, step, 0)
        sent(r6b.at[h], snd.at[h, 8])

    def j_(h):
        arrive(r6b.at[h], rcv.at[h, 8])
        gi = t * Y + y
        acc = s6b[h, pl.ds(pl.multiple_of(gi * pr, pr), pr), :].astype(F32)
        for n in range(G - 1):
            acc = acc + r6b[h, n * pr : (n + 1) * pr, :].astype(F32)
        value = pivot(acc, rfa, rfb, me * pr, pr).astype(BF)
        at = pl.ds(pl.multiple_of((k * G + gi) * pr, pr), pr)
        rsc[h, at, :] = value

        def step(n, carry):
            send(rsc.at[h, at], rsc.at[h, at], snd.at[h, 9], rcv.at[h, 9], g_id((gi + n) % G))
            return carry

        lax.fori_loop(1, G, step, 0)
        sent(rsc.at[h, pl.ds(0, (G - 1) * pr)], snd.at[h, 9])

    def k_(h):
        rh = RR // 2
        arrive(rsc.at[h, pl.ds(0, (G - 1) * pr)], rcv.at[h, 9])
        mine = pl.ds(k * rh, rh)
        send(rsc.at[h, mine], rsc.at[h, mine], snd.at[h, 10], rcv.at[h, 10], sib)
        sent(rsc.at[h, pl.ds(0, rh)], snd.at[h, 10])

    def l_(h):
        arrive(rsc.at[h, pl.ds(0, RR // 2)], rcv.at[h, 10])

        def fn(i):
            s8[h, pl.ds(i, MT), :] = nn(roott[pl.ds(i, MT), :], rsc[h]).astype(BF)

        tiled(RB, fn)
        z_scatter(h, s8, r8, pz, 11)

    def m_(h):
        z_gather(h, rs, z_sum(h, s8, r8, pz, 11).astype(BF), pz, 12)

    def n_(h):
        z_gathered(h, rs, pz, 12)
        exchange(h, asmt, rs, s10, r10, 13)
        out_r[:, h * W : (h + 1) * W] = rs[h]

    def o_(h):
        exchanged(h, r10, 13)

        def fn(i):
            s11[h, pl.ds(i, MT), :] = nn(ls[pl.ds(i, MT), :], r10[h]).astype(BF)

        halves(CR, fn, lambda: col_core_send(h, s11, r11, 14))
        sent(r11.at[h], snd.at[h, 14])

    def p_(h):
        col_y_send(h, s11, r11, s11b, r11b, 14)

    def q_(h):
        acc = col_sum(h, s11b, r11b, 14)
        value = jnp.where(live(h), scaled[h] - acc, 0.0).astype(BF)
        col_gather(h, res, value, 16, 1)

    def r_(h):
        col_forward(h, res, 16, 1)

    def s_(h):
        col_gathered(h, res, 16)

        def fn(i):
            s13[h, pl.ds(i, MT), :] = nn(invt[pl.ds(i, MT), :], res[h]).astype(BF)

        tiled(CC, fn)
        if RST:
            z_tree_scatter(h, s13, mid, r13, pu, 18)
        else:
            z_scatter(h, s13, r13, pu, 18)

    def s2_(h):
        if RST:
            z_tree_pass(h, s13, mid, r13, pu, 18)

    def t_(h):
        gather = z_tree if TREE else z_gather
        gather(h, cs, (z_tree_sum if RST else z_sum)(h, s13, r13, pu, 18).astype(BF), pu, 20)

    def t2_(h):
        if TREE:
            z_tree_forward(h, cs, pu, 20)

    def u_(h):
        arrive(cs.at[h, pl.ds(0, (Z - 3 if TREE else Z - 1) * pu)], rcv.at[h, 20])
        out_c[:, h * W : (h + 1) * W] = cs[h]

    def first(h):
        fn = a1(h)
        if h == 0:
            small_loads[7].wait()
            pl.semaphore_wait(barrier, Q - 1 + Z - 1)
        halves(CR, fn, lambda: col_core_send(h, s1, r1, 0))
        sent(r1.at[h], snd.at[h, 0])

    def coefs():
        for n in range(6):
            small_loads[n].wait()
        make_coefs()
        at = pl.ds(pl.multiple_of(k * half + y * pc, pc), pc)
        for h in range(H):
            scaled[h] = pivot(sol[h, at, :].astype(F32), cfa, cfb, c * pc, pc)

    small_loads[6].wait()
    make_slots()
    for n in range(3):
        loads[n].wait()
    mask_child()
    local = {
        "sel": make_sel,
        "meta": send_meta,
        "lst0": lambda: make_lst(0),
        "lst1": lambda: make_lst(1),
        "ident": make_ident,
        "asm": make_asm,
        "coefs": coefs,
        "mask": mask_root,
        "roott": lambda: transpose_into(root, roott, RR, RB, pr),
        "ls0": lambda: make_ls(0),
        "ls1": lambda: make_ls(1),
        "asmt": make_asmt,
        "invt": lambda: transpose_into(inv, invt, CR, CC, pc),
        "rrhs": loads[7].wait,
    }
    steps = [first, b, cc, d, e, f, g, hh, i_, j_, k_, l_, m_, n_, o_, p_, q_, r_, s_, s2_, t_, t2_, u_]
    names = dict(zip("abcdefghijklmnopqrsStTu", steps))
    for item in ORDER:
        if item in local:
            local[item]()
        else:
            names[item[0]](int(item[1]))
    for view, sem in pending:
        arrive(view, sem)


def shards(dims, *args):
    (child_inverse, child_lower, child_rhs, child_diag, child_off, child_pattern, child_pivots, child_map,
     root_inverse, root_rhs, root_diag, root_off, root_pattern) = args
    T, Z, Y, CR, CC, U, RB, RR, R, H = dims
    C, Q, G, W = Y * CORES, T * Y * CORES, T * Y, R // H
    NS = Q * CAP
    pc, pr, pz, pu = CR // C, RR // Q, RB // Z, CC // Z

    def chain(rows):
        return pltpu.VMEM((H, rows, W), BF)

    vm = lambda *shape: pltpu.VMEM(shape, BF)
    fm = lambda *shape: pltpu.VMEM(shape, F32)
    half = CR // 2
    scratch = [
        vm(C, pc, CC), vm(CC, CR), vm(C, pc, U), vm(NS, CR), vm(CR, NS), vm(NS, U), vm(Q, pr, RB), vm(RB, RR),
        vm(RB, NS), vm(NS, RB), vm(TILE, TILE), vm(CC, R), vm(RB, R),
        pltpu.VMEM((8, U), jnp.int32), fm(Q // 2, 8, 128), fm(Q, 8, 128),
        fm(max(pc, 128), 128), fm(max(pc, 128), 128), fm(max(pr, 128), 128), fm(max(pr, 128), 128), fm(H, pc, W),
        chain(CR), chain(half), chain(half), chain((Y - 1) * pc), chain(CR), chain(NS), chain(NS), chain(RB),
        chain((Z - 1) * pz), chain(RB),
        chain(RR), chain(RR // 2), chain(RR // 2), chain((G - 1) * pr), chain(RR), chain(RB), chain((Z - 1) * pz),
        chain(RB), chain(NS), chain(NS),
        chain(CR), chain(half), chain(half), chain((Y - 1) * pc), chain(CR), chain(CC), chain((Z - 1) * pu), chain(3 * pu), chain(CC),
        *[pltpu.VMEM((1, n), dt) for n, dt in ((CR, F32), (CR, F32), (CR, jnp.int32), (RR, F32), (RR, F32), (RR, jnp.int32), (U, jnp.int32), (1, jnp.int32))],
        pltpu.SemaphoreType.DMA((8,)), pltpu.SemaphoreType.DMA((8,)), pltpu.SemaphoreType.DMA((H, 21)), pltpu.SemaphoreType.DMA((H, 21)),
        pltpu.SemaphoreType.DMA((H, 2, Y - 1)), pltpu.SemaphoreType.DMA((H, 4)), pltpu.SemaphoreType.DMA((2,)),
    ]
    anyspec = pl.BlockSpec(memory_space=pl.ANY)
    vspec = pl.BlockSpec(memory_space=pltpu.VMEM)
    flops = 2 * R * (2 * CR * CC + 2 * NS * CR + 2 * RB * NS + 2 * RR * RB)
    child, rooted = pl.pallas_call(
        functools.partial(body, dims),
        name="substitution",
        out_shape=(OUT((CC, R), BF), OUT((RB, R), BF)),
        in_specs=[anyspec] * 13,
        out_specs=(vspec, vspec),
        scratch_shapes=scratch,
        cost_estimate=pl.CostEstimate(flops=flops, bytes_accessed=8 << 20, transcendentals=0),
        compiler_params=pltpu.CompilerParams(collective_id=0, has_side_effects=True, vmem_limit_bytes=58 << 20),
    )(
        child_inverse.reshape(Y, CORES, pc, CC),
        child_lower.reshape(Y, CORES, pc, U),
        root_inverse.reshape(G, CORES, pr, RB),
        child_rhs.reshape(CC, R),
        root_rhs,
        child_diag.reshape(1, CR),
        child_off.reshape(1, CR),
        child_pattern.reshape(1, CR),
        root_diag.reshape(1, RR),
        root_off.reshape(1, RR),
        root_pattern.reshape(1, RR),
        child_map.reshape(1, U),
        child_pivots.reshape(1, 1),
    )
    return (child.astype(F32)[None], rooted.astype(F32))


def solution(mesh):
    T, Z, C = mesh.shape["team"], mesh.shape["row"], mesh.shape["col"]

    def run(*args):
        pc_, uc = args[0].shape[1], args[1].shape[2]
        fr, R = args[9].shape
        dims = (T, Z, C // CORES, pc_ // Z, pc_ // C, uc // C, fr // (T * C), fr // Z, R, CHAINS)
        return jax.shard_map(
            functools.partial(shards, dims),
            mesh=mesh,
            in_specs=(
                P("team", "row", "col"),
                P("team", "row", "col"),
                P("team", "col", None),
                P("team", "row"),
                P("team", "row"),
                P("team", "row"),
                P("team"),
                P("team", "col"),
                P("row", ("team", "col")),
                P(("team", "col"), None),
                P("row"),
                P("row"),
                P("row"),
            ),
            out_specs=(P("team", "col", None), P(("team", "col"), None)),
            check_vma=False,
        )(*args)

    return run
```

```python
import functools

import jax
import jax.numpy as jnp
from jax import lax
from jax.experimental import pallas as pl
from jax.experimental.pallas import tpu as pltpu
from jax.sharding import PartitionSpec as P

BF = jnp.bfloat16
F32 = jnp.float32
MESH = pl.DeviceIdType.MESH
CORES = 2
CAP = 64
TILE = 256
MT = 512
XT = 256
CHAINS = 2
ORDER = ["sel", "b0", "b1", "meta", "lst0", "c0", "c1", "ident", "lst1", "d0", "e0", "d1"]
ORDER += ["asm", "coefs", "mask", "e1", "roott", "f0", "rrhs", "f1", "g0", "g1", "h0", "i0", "h1", "i1", "j0", "asmt"]
ORDER += ["j1", "k0", "l0", "k1", "l1", "ls0", "m0", "ls1", "m1", "n0", "n1", "invt", "o0", "p0", "o1", "q0", "p1"]
ORDER += ["r0", "q1", "s0", "r1", "s1", "S0", "S1", "t0", "t1", "T0", "T1", "u0", "u1"]
TREE = True
RST = False
ZH = False
OUT = pltpu.VMEM


def nn(a, b):
    return jnp.dot(a, b, preferred_element_type=F32)


def nt(a, b):
    return lax.dot_general(a, b, (((1,), (1,)), ((), ())), preferred_element_type=F32)


def body(dims, *refs):
    T, Z, Y, CR, CC, U, RB, RR, R, H = dims
    C = Y * CORES
    Q = T * C
    G = T * Y
    W = R // H
    NS = Q * CAP
    pc, pr, pz, pu = CR // C, RR // Q, RB // Z, CC // Z
    it = iter(refs)
    take = lambda n: [next(it) for _ in range(n)]
    inv_h, low_h, root_h, rhs_h, rrhs_h = take(5)
    small_h = take(8)
    out_c, out_r = take(2)
    inv, invt, low, lst, ls, sel, root, roott, asm, asmt, ident, rhs, rrhs = take(13)
    slot, msend, mrecv, cfa, cfb, rfa, rfb, scaled = take(8)
    s1, r1, s2, r2, sol, s3, r3, s4, r4, upd = take(10)
    s6, r6, s6b, r6b, rsc, s8, r8, rs, s10, r10 = take(10)
    s11, r11, s11b, r11b, res, s13, r13, mid, cs = take(9)
    small = take(8)
    cdiag, coff, cpat, rdiag, roff, rpat, cmap, piv = small
    in_sem, small_sem, snd, rcv, ysem, zsem, msem = take(7)

    t = lax.axis_index("team")
    r = lax.axis_index("row")
    c = lax.axis_index("col")
    y = c // CORES
    k = c % CORES
    me = t * C + c
    sib = (t, r, y * CORES + (1 - k))

    def plane_id(q):
        return (t * 0 + q // C, r, q % C)

    def z_id(d):
        return (t, (r + d) % Z, c)

    def y_id(d):
        return (t, r, ((y + d) % Y) * CORES + k)

    def g_id(g):
        return (g // Y, r, (g % Y) * CORES + k)

    barrier = pltpu.get_barrier_semaphore()

    def greet_plane(d, carry):
        pl.semaphore_signal(barrier, inc=1, device_id=plane_id((me + d) % Q), device_id_type=MESH)
        return carry

    def greet_z(d, carry):
        pl.semaphore_signal(barrier, inc=1, device_id=z_id(d), device_id_type=MESH)
        return carry

    loads = [pltpu.make_async_copy(rhs_h, rhs, in_sem.at[0])]
    for kk in range(CORES):
        loads.append(pltpu.make_async_copy(inv_h.at[:, kk], inv.at[pl.ds(kk * Y, Y)], in_sem.at[1 + kk]))
    for kk in range(CORES):
        loads.append(pltpu.make_async_copy(low_h.at[:, kk], low.at[pl.ds(kk * Y, Y)], in_sem.at[3 + kk]))
    for kk in range(CORES):
        loads.append(pltpu.make_async_copy(root_h.at[:, kk], root.at[pl.ds(kk * G, G)], in_sem.at[5 + kk]))
    loads.append(pltpu.make_async_copy(rrhs_h, rrhs, in_sem.at[7]))
    small_loads = [pltpu.make_async_copy(a, b, small_sem.at[n]) for n, (a, b) in enumerate(zip(small_h, small))]
    small_loads[6].start()
    for ld in loads[:3]:
        ld.start()
    lax.fori_loop(1, Q, greet_plane, 0)
    lax.fori_loop(1, Z, greet_z, 0)
    for ld in small_loads[7:] + loads[3:] + small_loads[:6]:
        ld.start()

    def send(src, dst, sem_s, sem_r, dev):
        pltpu.make_async_remote_copy(
            src_ref=src, dst_ref=dst, send_sem=sem_s, recv_sem=sem_r, device_id=dev, device_id_type=MESH
        ).start()

    def arrive(view, sem):
        pltpu.make_async_copy(view, view, sem).wait()

    pending = []

    def sent(view, sem):
        pending.append((view, sem))

    def cols(h):
        return pl.ds(h * W, W)

    def halves(n, fn, push):
        def step(i, carry):
            fn(pl.multiple_of(((1 - k) * (n // 2 // MT) + i) % (n // MT) * MT, MT))

            @pl.when(i == n // 2 // MT - 1)
            def _():
                push()

            return carry

        lax.fori_loop(0, n // MT, step, 0)

    def tiled(n, fn, tile=MT):
        def step(i, carry):
            fn(pl.multiple_of(i * tile, tile))
            return carry

        lax.fori_loop(0, n // tile, step, 0)

    def mask_child():
        @pl.when(c > r)
        def _():
            def step(p, carry):
                inv[p] = jnp.zeros((pc, CC), BF)
                return carry

            lax.fori_loop(0, C, step, 0)

        @pl.when(c == r)
        def _():
            rows = lax.broadcasted_iota(jnp.int32, (pc, pc), 0)
            colid = lax.broadcasted_iota(jnp.int32, (pc, pc), 1)
            for p in range(C):
                at = ((p % Y) * CORES + p // Y) * pc
                blk = inv[p, :, at : at + pc].astype(F32)
                blk = jnp.where(colid < rows, blk, jnp.where(colid == rows, 1.0, 0.0))
                inv[p, :, at : at + pc] = blk.astype(BF)
                if at + pc < CC:
                    inv[p, :, at + pc :] = jnp.zeros((pc, CC - at - pc), BF)

    def mask_root():
        for kk in range(2):
            loads[5 + kk].wait()

        @pl.when(me * RB + RB > r * RR)
        def _():
            def step(p, carry):
                g = p % G
                piece = (g // Y) * C + (g % Y) * CORES + p // G
                rows = r * RR + piece * pr + lax.broadcasted_iota(jnp.int32, (pr, RB), 0)
                colid = me * RB + lax.broadcasted_iota(jnp.int32, (pr, RB), 1)
                blk = root[p].astype(F32)
                blk = jnp.where(colid < rows, blk, jnp.where(colid == rows, 1.0, 0.0))
                root[p] = blk.astype(BF)
                return carry

            lax.fori_loop(0, 2 * G, step, 0)

    def make_ident():
        a = lax.broadcasted_iota(jnp.int32, (TILE, TILE), 0)
        b = lax.broadcasted_iota(jnp.int32, (TILE, TILE), 1)
        ident[...] = jnp.where(a == b, 1.0, 0.0).astype(BF)

    def transpose_into(x, xt, m, n, per):
        mt = min(512, m)
        for j in range(n // TILE):

            def step(i, carry):
                blk = x[pl.ds(i * (mt // per), mt // per), :, pl.ds(j * TILE, TILE)].reshape(mt, TILE)
                xt[pl.ds(j * TILE, TILE), pl.ds(pl.multiple_of(i * mt, mt), mt)] = nt(ident[...], blk).astype(BF)
                return carry

            lax.fori_loop(0, m // mt, step, 0)

    def make_slots():
        a = lax.broadcasted_iota(jnp.int32, (128, 128), 0)
        b = lax.broadcasted_iota(jnp.int32, (128, 128), 1)
        tri = jnp.where(a <= b, 1.0, 0.0).astype(BF)
        own_id = lax.broadcasted_iota(jnp.int32, (Q, 128), 0)
        base = jnp.zeros((Q, 1), F32)
        for i in range(U // 128):
            m = jnp.broadcast_to(cmap[:, i * 128 : (i + 1) * 128], (Q, 128))
            owner = m // RB
            hot = jnp.where(owner == own_id, 1.0, 0.0)
            count = nn(hot.astype(BF), tri)
            rank = jnp.sum(hot * (count + base - 1.0), axis=0, keepdims=True)
            base = base + jnp.sum(hot, axis=1, keepdims=True)
            slot[:, i * 128 : (i + 1) * 128] = jnp.broadcast_to(
                owner[0:8] * CAP + rank.astype(jnp.int32), (8, 128)
            )

    def make_sel():
        off = cmap[...] % RB
        row = lax.broadcasted_iota(jnp.int32, (16, U), 0)
        offb = jnp.broadcast_to(off, (16, U))
        probe = jnp.where(row == 0, offb // 16, jnp.where(row == 1, offb % 16, 1))
        probe = jnp.where(row < 3, probe, 0).astype(F32).astype(BF)

        def step(i, carry):
            ids = i * TILE + lax.broadcasted_iota(jnp.int32, (TILE, U), 0)
            blk = jnp.where(ids == slot[0:1, :], 1.0, 0.0).astype(BF)
            sel[pl.ds(pl.multiple_of(i * TILE, TILE), TILE), :] = blk
            info = nt(probe, blk)
            val = jnp.where(info[2:3] > 0.5, info[0:1] * 16.0 + info[1:2], float(RB))
            for j in range(TILE // 128):
                msend[i * (TILE // 128) + j] = jnp.broadcast_to(val[:, j * 128 : (j + 1) * 128], (8, 128))
            return carry

        lax.fori_loop(0, NS // TILE, step, 0)

    def send_meta():
        def step(d, carry):
            q = (me + d) % Q
            send(msend.at[q // 2], mrecv.at[me], msem.at[0], msem.at[1], plane_id(q))
            return carry

        lax.fori_loop(1, Q, step, 0)
        sent(mrecv.at[pl.ds(0, Q - 1)], msem.at[0])
        mrecv[me] = msend[me // 2]

    def make_lst(part_no):
        if part_no == 0:
            for kk in range(2):
                loads[3 + kk].wait()

        def step(i, carry):
            at = pl.ds(pl.multiple_of(i * TILE, TILE), TILE)
            blk = sel[at, :]
            for j in range(CR // 512):
                part = low[pl.ds(j * (512 // pc), 512 // pc)].reshape(512, U)
                lst[at, j * 512 : (j + 1) * 512] = nt(blk, part).astype(BF)
            return carry

        count = NS // TILE // 2
        lax.fori_loop(part_no * count, (part_no + 1) * count, step, 0)

    def make_ls(part_no):
        def step(i, carry):
            part = low[pl.ds(i * (TILE // pc), TILE // pc)].reshape(TILE, U)
            at = pl.ds(pl.multiple_of(i * TILE, TILE), TILE)
            for j in range(NS // 512):
                ls[at, j * 512 : (j + 1) * 512] = nt(part, sel[j * 512 : (j + 1) * 512, :]).astype(BF)
            return carry

        count = CR // TILE // 2
        lax.fori_loop(part_no * count, (part_no + 1) * count, step, 0)

    def make_asm():
        arrive(mrecv.at[pl.ds(0, Q - 1)], msem.at[1])

        def step(j, carry):
            lane = lax.broadcasted_iota(jnp.int32, (8, 128), 1)
            a, b = mrecv[2 * j], mrecv[2 * j + 1]
            ar, br = pltpu.roll(a, 64, 1), pltpu.roll(b, 64, 1)
            first = jnp.where(lane < 64, a, br)
            second = jnp.where(lane < 64, ar, b)
            kf = k.astype(F32)
            val = first * (1.0 - kf) + second * kf
            ids = lax.broadcasted_iota(jnp.int32, (RB, 128), 0).astype(F32)
            blk = jnp.where(ids == val[0:1, :], 1.0, 0.0).astype(BF)
            asm[:, pl.ds(pl.multiple_of(j * 128, 128), 128)] = blk
            return carry

        lax.fori_loop(0, Q // 2, step, 0)

    def make_asmt():
        def step(i, carry):
            at = pl.multiple_of(i * TILE, TILE)
            asmt[pl.ds(at, TILE), :] = nt(ident[...], asm[:, pl.ds(at, TILE)]).astype(BF)
            return carry

        lax.fori_loop(0, NS // TILE, step, 0)

    def coefficients(dref, oref, pref, fa, fb, start, n):
        first = (start // 128) * 128
        lane = lax.broadcasted_iota(jnp.int32, (128, 128), 1)
        even = lane % 2 == 0
        for i in range(max(1, n // 128)):
            at = pl.ds(pl.multiple_of(first + i * 128, 128), 128)
            a = jnp.broadcast_to(dref[:, at], (128, 128))
            o = jnp.broadcast_to(oref[:, at], (128, 128))
            p = jnp.broadcast_to(pref[:, at], (128, 128))
            partner = jnp.where(even, pltpu.roll(a, 127, 1), pltpu.roll(a, 1, 1))
            coup = jnp.where(p == 1, o, 0.0)
            coup = jnp.where(even, coup, pltpu.roll(coup, 1, 1))
            det = a * partner - coup * coup
            fa[pl.ds(i * 128, 128), :] = (partner / det).T
            fb[pl.ds(i * 128, 128), :] = (-coup / det).T

    def pivot(v, fa, fb, start, n):
        at = pl.ds(0, n) if n >= 128 else pl.ds(pl.multiple_of(start % 128, n), n)
        a = jnp.concatenate([fa[at, :]] * (W // 128), axis=1)
        b = jnp.concatenate([fb[at, :]] * (W // 128), axis=1)
        even = lax.broadcasted_iota(jnp.int32, (n, W), 0) % 2 == 0
        partner = jnp.where(even, pltpu.roll(v, n - 1, 0), pltpu.roll(v, 1, 0))
        return a * v + b * partner

    def make_coefs():
        coefficients(cdiag, coff, cpat, cfa, cfb, c * pc, pc)
        coefficients(rdiag, roff, rpat, rfa, rfb, me * pr, pr)

    def away(i, size):
        return size // 2 + (1 - 2 * (i % 2)) * ((i + 1) // 2)

    half = CR // 2

    def col_core_send(h, s_a, r_a, st):
        send(s_a.at[h, pl.ds((1 - k) * half, half)], r_a.at[h], snd.at[h, st], rcv.at[h, st], sib)

    def col_y_send(h, s_a, r_a, s_b, r_b, st):
        arrive(r_a.at[h], rcv.at[h, st])
        s_b[h] = (s_a[h, pl.ds(pl.multiple_of(k * half, half), half), :].astype(F32) + r_a[h].astype(F32)).astype(BF)
        for d in [away(n, Y) for n in range(Y - 1)]:
            p = (y + d) % Y
            send(s_b.at[h, pl.ds(p * pc, pc)], r_b.at[h, pl.ds((d - 1) * pc, pc)], snd.at[h, st + 1], rcv.at[h, st + 1], y_id(d))
        sent(r_b.at[h], snd.at[h, st + 1])

    def col_sum(h, s_b, r_b, st):
        arrive(r_b.at[h], rcv.at[h, st + 1])
        acc = s_b[h, pl.ds(pl.multiple_of(y * pc, pc), pc), :].astype(F32)
        for d in range(Y - 1):
            acc = acc + r_b[h, d * pc : (d + 1) * pc, :].astype(F32)
        return acc

    def col_gather(h, buf, value, st, ys):
        at = pl.ds(pl.multiple_of(k * half + y * pc, pc), pc)
        buf[h, at, :] = value
        for d in [away(n, Y) for n in range(Y - 1)]:
            send(buf.at[h, at], buf.at[h, at], snd.at[h, st], ysem.at[h, ys, d - 1], y_id(d))
        send(buf.at[h, at], buf.at[h, at], snd.at[h, st + 1], rcv.at[h, st + 1], sib)
        sent(buf.at[h, pl.ds(0, (Y - 1) * pc)], snd.at[h, st])
        sent(buf.at[h, pl.ds(0, half)], snd.at[h, st + 1])

    def col_forward(h, buf, st, ys):
        for d in (1, Y - 1, 2) if Y == 4 else range(1, Y):
            at = pl.ds(pl.multiple_of(k * half + ((y + Y - d) % Y) * pc, pc), pc)
            arrive(buf.at[h, at], ysem.at[h, ys, d - 1])
            send(buf.at[h, at], buf.at[h, at], snd.at[h, st + 1], rcv.at[h, st + 1], sib)

    def col_gathered(h, buf, st):
        arrive(buf.at[h, pl.ds(0, half)], rcv.at[h, st + 1])

    def far(i):
        return away(i, Z)

    def chip(n):
        return (t + away(n // Y, T)) % T * Y + (y + away(n % Y, Y)) % Y

    def z_scatter(h, s, rr, n, st):
        def step(i, carry):
            d = far(i)
            to = (r + d) % Z
            send(s.at[h, pl.ds(to * n, n)], rr.at[h, pl.ds((d - 1) * n, n)], snd.at[h, st], rcv.at[h, st], z_id(d))
            return carry

        lax.fori_loop(0, Z - 1, step, 0)
        sent(rr.at[h], snd.at[h, st])

    def z_product(h, mat, vec, s, rr, n, st):
        side = Z // 2
        rows = side * n

        def step(i, carry):
            g = (r // side + 1 + i) % 2
            at = pl.multiple_of(g * rows, rows)
            s[h, pl.ds(at, rows), :] = nn(mat[pl.ds(at, rows), :], vec[h]).astype(BF)
            for j in range(side):
                to = g * side + j

                @pl.when(to != r)
                def _():
                    d = (to - r + Z) % Z
                    send(s.at[h, pl.ds(to * n, n)], rr.at[h, pl.ds((d - 1) * n, n)], snd.at[h, st], rcv.at[h, st], (t, to, c))

            return carry

        lax.fori_loop(0, 2, step, 0)
        sent(rr.at[h], snd.at[h, st])

    def z_sum(h, s, rr, n, st):
        arrive(rr.at[h], rcv.at[h, st])
        acc = s[h, pl.ds(pl.multiple_of(r * n, n), n), :].astype(F32)
        for d in range(Z - 1):
            acc = acc + rr[h, d * n : (d + 1) * n, :].astype(F32)
        return acc

    def z_gather(h, buf, value, n, st):
        at = pl.ds(pl.multiple_of(r * n, n), n)
        buf[h, at, :] = value

        def step(i, carry):
            send(buf.at[h, at], buf.at[h, at], snd.at[h, st], rcv.at[h, st], z_id(far(i)))
            return carry

        lax.fori_loop(0, Z - 1, step, 0)
        sent(buf.at[h, pl.ds(0, (Z - 1) * n)], snd.at[h, st])

    def z_gathered(h, buf, n, st):
        arrive(buf.at[h, pl.ds(0, (Z - 1) * n)], rcv.at[h, st])

    def z_tree_scatter(h, s, mid, rr, n, st):
        def part(to):
            return s.at[h, pl.ds(((r + to) % Z) * n, n)]

        for i, (to, via) in enumerate(((3, 1), (Z - 3, Z - 1), (4, (2, Z - 2)[h % 2]))):
            sem = zsem.at[h, 2 + (i if i < 2 else h % 2)]
            send(part(to), mid.at[h, pl.ds(i * n, n)], snd.at[h, st], sem, z_id(via))
        for i, to in enumerate((1, Z - 1)):
            send(part(to), rr.at[h, pl.ds(i * n, n)], snd.at[h, st], rcv.at[h, st], z_id(to))
        sent(s.at[h, pl.ds(0, 5 * n)], snd.at[h, st])

    def z_tree_pass(h, s, mid, rr, n, st):
        for i, to in enumerate((2, Z - 2)):
            both = i == h % 2
            view = mid.at[h, pl.ds(0, (2 if both else 1) * n)]
            arrive(view, zsem.at[h, 2 + i])
            at = pl.ds(pl.multiple_of(((r + to) % Z) * n, n), n)
            acc = s[h, at, :].astype(F32) + mid[h, i * n : (i + 1) * n, :].astype(F32)
            if both:
                acc = acc + mid[h, 2 * n : 3 * n, :].astype(F32)
            s[h, at, :] = acc.astype(BF)
            send(s.at[h, at], rr.at[h, pl.ds((2 + i) * n, n)], snd.at[h, st + 1], rcv.at[h, st], z_id(to))
        sent(s.at[h, pl.ds(0, 2 * n)], snd.at[h, st + 1])

    def z_tree_sum(h, s, rr, n, st):
        arrive(rr.at[h, pl.ds(0, 4 * n)], rcv.at[h, st])
        acc = s[h, pl.ds(pl.multiple_of(r * n, n), n), :].astype(F32)
        for d in range(4):
            acc = acc + rr[h, d * n : (d + 1) * n, :].astype(F32)
        return acc

    def z_tree(h, buf, value, n, st):
        at = pl.ds(pl.multiple_of(r * n, n), n)
        buf[h, at, :] = value
        for i, d in enumerate((2, Z - 2)):
            send(buf.at[h, at], buf.at[h, at], snd.at[h, st], zsem.at[h, i], z_id(d))
        for d in (1, Z - 1):
            send(buf.at[h, at], buf.at[h, at], snd.at[h, st], rcv.at[h, st], z_id(d))
        sent(buf.at[h, pl.ds(0, (Z - 1) * n)], snd.at[h, st])

    def z_tree_forward(h, buf, n, st):
        for i, d in enumerate((2, Z - 2)):
            at = pl.ds(pl.multiple_of(((r + Z - d) % Z) * n, n), n)
            arrive(buf.at[h, at], zsem.at[h, i])
            if i == h % 2:
                send(buf.at[h, at], buf.at[h, at], snd.at[h, st], rcv.at[h, st], z_id(d))
            send(buf.at[h, at], buf.at[h, at], snd.at[h, st], rcv.at[h, st], z_id((1, Z - 1)[i]))

    def exchange(h, mat, vec, s, rr, st):
        per = XT // CAP
        groups = NS // XT

        def step(i, carry):
            g = (me // per + 1 + i) % groups
            at = pl.multiple_of(g * XT, XT)
            s[h, pl.ds(at, XT), :] = nn(mat[pl.ds(at, XT), :], vec[h]).astype(BF)
            for j in range(per):
                q = g * per + j

                @pl.when(q != me)
                def _():
                    send(s.at[h, pl.ds(q * CAP, CAP)], rr.at[h, pl.ds(me * CAP, CAP)], snd.at[h, st], rcv.at[h, st], plane_id(q))

            return carry

        lax.fori_loop(0, groups, step, 0)
        sent(rr.at[h, pl.ds(0, NS - CAP)], snd.at[h, st])
        at = pl.ds(pl.multiple_of(me * CAP, CAP), CAP)
        rr[h, at, :] = s[h, at, :]

    def exchanged(h, rr, st):
        arrive(rr.at[h, pl.ds(0, NS - CAP)], rcv.at[h, st])

    def live(h):
        rows = r * CR + c * pc + lax.broadcasted_iota(jnp.int32, (pc, W), 0)
        return rows < piv[...]

    def b(h):
        col_y_send(h, s1, r1, s2, r2, 0)

    def cc(h):
        acc = col_sum(h, s2, r2, 0)
        solved = jnp.where(live(h), acc, 0.0).astype(BF)
        col_gather(h, sol, solved, 2, 0)

    def d(h):
        col_forward(h, sol, 2, 0)

    def e(h):
        col_gathered(h, sol, 2)
        exchange(h, lst, sol, s3, r3, 4)

    def f(h):
        exchanged(h, r3, 4)
        if ZH:
            z_product(h, asm, r3, s4, r4, pz, 5)
            return

        def fn(i):
            s4[h, pl.ds(i, MT), :] = nn(asm[pl.ds(i, MT), :], r3[h]).astype(BF)

        tiled(RB, fn)
        z_scatter(h, s4, r4, pz, 5)

    def g(h):
        acc = z_sum(h, s4, r4, pz, 5)
        mine = rrhs[pl.ds(pl.multiple_of(r * pz, pz), pz), h * W : (h + 1) * W].astype(F32)
        z_gather(h, upd, (mine - acc).astype(BF), pz, 6)

    def hh(h):
        z_gathered(h, upd, pz, 6)

        def fn(i):
            tile = root[pl.ds(i // pr, MT // pr)].reshape(MT, RB)
            s6[h, pl.ds(i, MT), :] = nn(tile, upd[h]).astype(BF)

        rh = RR // 2
        halves(RR, fn, lambda: send(s6.at[h, pl.ds((1 - k) * rh, rh)], r6.at[h], snd.at[h, 7], rcv.at[h, 7], sib))
        sent(r6.at[h], snd.at[h, 7])

    def i_(h):
        arrive(r6.at[h], rcv.at[h, 7])
        rh = RR // 2
        gi = t * Y + y

        def step(j, carry):
            p = chip(j)
            at = pl.ds(pl.multiple_of(p * pr, pr), pr)
            mine = pl.ds(pl.multiple_of(k * rh + p * pr, pr), pr)
            s6b[h, at, :] = (s6[h, mine, :].astype(F32) + r6[h, at, :].astype(F32)).astype(BF)

            @pl.when(p != gi)
            def _():
                send(s6b.at[h, at], r6b.at[h, pl.ds(j * pr, pr)], snd.at[h, 8], rcv.at[h, 8], g_id(p))

            return carry

        lax.fori_loop(0, G, step, 0)
        sent(r6b.at[h], snd.at[h, 8])

    def j_(h):
        arrive(r6b.at[h], rcv.at[h, 8])
        gi = t * Y + y
        acc = s6b[h, pl.ds(pl.multiple_of(gi * pr, pr), pr), :].astype(F32)
        for n in range(G - 1):
            acc = acc + r6b[h, n * pr : (n + 1) * pr, :].astype(F32)
        value = pivot(acc, rfa, rfb, me * pr, pr).astype(BF)
        at = pl.ds(pl.multiple_of((k * G + gi) * pr, pr), pr)
        rsc[h, at, :] = value

        def step(n, carry):
            send(rsc.at[h, at], rsc.at[h, at], snd.at[h, 9], rcv.at[h, 9], g_id(chip(n - 1)))
            return carry

        lax.fori_loop(1, G, step, 0)
        sent(rsc.at[h, pl.ds(0, (G - 1) * pr)], snd.at[h, 9])

    def k_(h):
        rh = RR // 2
        arrive(rsc.at[h, pl.ds(0, (G - 1) * pr)], rcv.at[h, 9])
        mine = pl.ds(k * rh, rh)
        send(rsc.at[h, mine], rsc.at[h, mine], snd.at[h, 10], rcv.at[h, 10], sib)
        sent(rsc.at[h, pl.ds(0, rh)], snd.at[h, 10])

    def l_(h):
        arrive(rsc.at[h, pl.ds(0, RR // 2)], rcv.at[h, 10])
        if ZH:
            z_product(h, roott, rsc, s8, r8, pz, 11)
            return

        def fn(i):
            s8[h, pl.ds(i, MT), :] = nn(roott[pl.ds(i, MT), :], rsc[h]).astype(BF)

        tiled(RB, fn)
        z_scatter(h, s8, r8, pz, 11)

    def m_(h):
        z_gather(h, rs, z_sum(h, s8, r8, pz, 11).astype(BF), pz, 12)

    def n_(h):
        z_gathered(h, rs, pz, 12)
        exchange(h, asmt, rs, s10, r10, 13)
        out_r[:, h * W : (h + 1) * W] = rs[h]

    def o_(h):
        exchanged(h, r10, 13)

        def fn(i):
            s11[h, pl.ds(i, MT), :] = nn(ls[pl.ds(i, MT), :], r10[h]).astype(BF)

        halves(CR, fn, lambda: col_core_send(h, s11, r11, 14))
        sent(r11.at[h], snd.at[h, 14])

    def p_(h):
        col_y_send(h, s11, r11, s11b, r11b, 14)

    def q_(h):
        acc = col_sum(h, s11b, r11b, 14)
        value = jnp.where(live(h), scaled[h] - acc, 0.0).astype(BF)
        col_gather(h, res, value, 16, 1)

    def r_(h):
        col_forward(h, res, 16, 1)

    def s_(h):
        col_gathered(h, res, 16)
        if ZH:
            z_product(h, invt, res, s13, r13, pu, 18)
            return

        def fn(i):
            s13[h, pl.ds(i, MT), :] = nn(invt[pl.ds(i, MT), :], res[h]).astype(BF)

        tiled(CC, fn)
        if RST:
            z_tree_scatter(h, s13, mid, r13, pu, 18)
        else:
            z_scatter(h, s13, r13, pu, 18)

    def s2_(h):
        if RST:
            z_tree_pass(h, s13, mid, r13, pu, 18)

    def t_(h):
        gather = z_tree if TREE else z_gather
        gather(h, cs, (z_tree_sum if RST else z_sum)(h, s13, r13, pu, 18).astype(BF), pu, 20)

    def t2_(h):
        if TREE:
            z_tree_forward(h, cs, pu, 20)

    def u_(h):
        arrive(cs.at[h, pl.ds(0, (Z - 3 if TREE else Z - 1) * pu)], rcv.at[h, 20])
        out_c[:, h * W : (h + 1) * W] = cs[h]

    def first(start):
        def fn(i):
            at = pl.multiple_of(start + i, MT)
            value = nn(inv[pl.ds(at // pc, MT // pc)].reshape(MT, CC), rhs[...]).astype(BF)
            for h in range(H):
                s1[h, pl.ds(at, MT), :] = value[:, h * W : (h + 1) * W]

        tiled(half, fn)

    def coefs():
        for n in range(6):
            small_loads[n].wait()
        make_coefs()
        at = pl.ds(pl.multiple_of(k * half + y * pc, pc), pc)
        for h in range(H):
            scaled[h] = pivot(sol[h, at, :].astype(F32), cfa, cfb, c * pc, pc)

    small_loads[6].wait()
    make_slots()
    for n in range(3):
        loads[n].wait()
    mask_child()
    first((1 - k) * half)
    small_loads[7].wait()
    pl.semaphore_wait(barrier, Q - 1 + Z - 1)
    for h in range(H):
        col_core_send(h, s1, r1, 0)
        sent(r1.at[h], snd.at[h, 0])
    first(k * half)
    local = {
        "sel": make_sel,
        "meta": send_meta,
        "lst0": lambda: make_lst(0),
        "lst1": lambda: make_lst(1),
        "ident": make_ident,
        "asm": make_asm,
        "coefs": coefs,
        "mask": mask_root,
        "roott": lambda: transpose_into(root, roott, RR, RB, pr),
        "ls0": lambda: make_ls(0),
        "ls1": lambda: make_ls(1),
        "asmt": make_asmt,
        "invt": lambda: transpose_into(inv, invt, CR, CC, pc),
        "rrhs": loads[7].wait,
    }
    steps = [b, cc, d, e, f, g, hh, i_, j_, k_, l_, m_, n_, o_, p_, q_, r_, s_, s2_, t_, t2_, u_]
    names = dict(zip("bcdefghijklmnopqrsStTu", steps))
    for item in ORDER:
        if item in local:
            local[item]()
        else:
            names[item[0]](int(item[1]))
    for view, sem in pending:
        arrive(view, sem)


def shards(dims, *args):
    (child_inverse, child_lower, child_rhs, child_diag, child_off, child_pattern, child_pivots, child_map,
     root_inverse, root_rhs, root_diag, root_off, root_pattern) = args
    T, Z, Y, CR, CC, U, RB, RR, R, H = dims
    C, Q, G, W = Y * CORES, T * Y * CORES, T * Y, R // H
    NS = Q * CAP
    pc, pr, pz, pu = CR // C, RR // Q, RB // Z, CC // Z

    def chain(rows):
        return pltpu.VMEM((H, rows, W), BF)

    vm = lambda *shape: pltpu.VMEM(shape, BF)
    fm = lambda *shape: pltpu.VMEM(shape, F32)
    half = CR // 2
    scratch = [
        vm(C, pc, CC), vm(CC, CR), vm(C, pc, U), vm(NS, CR), vm(CR, NS), vm(NS, U), vm(Q, pr, RB), vm(RB, RR),
        vm(RB, NS), vm(NS, RB), vm(TILE, TILE), vm(CC, R), vm(RB, R),
        pltpu.VMEM((8, U), jnp.int32), fm(Q // 2, 8, 128), fm(Q, 8, 128),
        fm(max(pc, 128), 128), fm(max(pc, 128), 128), fm(max(pr, 128), 128), fm(max(pr, 128), 128), fm(H, pc, W),
        chain(CR), chain(half), chain(half), chain((Y - 1) * pc), chain(CR), chain(NS), chain(NS), chain(RB),
        chain((Z - 1) * pz), chain(RB),
        chain(RR), chain(RR // 2), chain(RR // 2), chain((G - 1) * pr), chain(RR), chain(RB), chain((Z - 1) * pz),
        chain(RB), chain(NS), chain(NS),
        chain(CR), chain(half), chain(half), chain((Y - 1) * pc), chain(CR), chain(CC), chain((Z - 1) * pu), chain(3 * pu), chain(CC),
        *[pltpu.VMEM((1, n), dt) for n, dt in ((CR, F32), (CR, F32), (CR, jnp.int32), (RR, F32), (RR, F32), (RR, jnp.int32), (U, jnp.int32), (1, jnp.int32))],
        pltpu.SemaphoreType.DMA((8,)), pltpu.SemaphoreType.DMA((8,)), pltpu.SemaphoreType.DMA((H, 21)), pltpu.SemaphoreType.DMA((H, 21)),
        pltpu.SemaphoreType.DMA((H, 2, Y - 1)), pltpu.SemaphoreType.DMA((H, 4)), pltpu.SemaphoreType.DMA((2,)),
    ]
    anyspec = pl.BlockSpec(memory_space=pl.ANY)
    vspec = pl.BlockSpec(memory_space=pltpu.VMEM)
    flops = 2 * R * (2 * CR * CC + 2 * NS * CR + 2 * RB * NS + 2 * RR * RB)
    child, rooted = pl.pallas_call(
        functools.partial(body, dims),
        name="substitution",
        out_shape=(OUT((CC, R), BF), OUT((RB, R), BF)),
        in_specs=[anyspec] * 13,
        out_specs=(vspec, vspec),
        scratch_shapes=scratch,
        cost_estimate=pl.CostEstimate(flops=flops, bytes_accessed=8 << 20, transcendentals=0),
        compiler_params=pltpu.CompilerParams(collective_id=0, has_side_effects=True, vmem_limit_bytes=58 << 20),
    )(
        child_inverse.reshape(Y, CORES, pc, CC),
        child_lower.reshape(Y, CORES, pc, U),
        root_inverse.reshape(G, CORES, pr, RB),
        child_rhs.reshape(CC, R),
        root_rhs,
        child_diag.reshape(1, CR),
        child_off.reshape(1, CR),
        child_pattern.reshape(1, CR),
        root_diag.reshape(1, RR),
        root_off.reshape(1, RR),
        root_pattern.reshape(1, RR),
        child_map.reshape(1, U),
        child_pivots.reshape(1, 1),
    )
    return (child.astype(F32)[None], rooted.astype(F32))


def solution(mesh):
    T, Z, C = mesh.shape["team"], mesh.shape["row"], mesh.shape["col"]

    def run(*args):
        pc_, uc = args[0].shape[1], args[1].shape[2]
        fr, R = args[9].shape
        dims = (T, Z, C // CORES, pc_ // Z, pc_ // C, uc // C, fr // (T * C), fr // Z, R, CHAINS)
        return jax.shard_map(
            functools.partial(shards, dims),
            mesh=mesh,
            in_specs=(
                P("team", "row", "col"),
                P("team", "row", "col"),
                P("team", "col", None),
                P("team", "row"),
                P("team", "row"),
                P("team", "row"),
                P("team"),
                P("team", "col"),
                P("row", ("team", "col")),
                P(("team", "col"), None),
                P("row"),
                P("row"),
                P("row"),
            ),
            out_specs=(P("team", "col", None), P(("team", "col"), None)),
            check_vma=False,
        )(*args)

    return run
```

```python
import functools

import jax
import jax.numpy as jnp
from jax import lax
from jax.experimental import pallas as pl
from jax.experimental.pallas import tpu as pltpu
from jax.sharding import PartitionSpec as P

BF = jnp.bfloat16
F32 = jnp.float32
MESH = pl.DeviceIdType.MESH
CORES = 2
CAP = 64
TILE = 256
MT = 512
XT = 256
CHAINS = 2
ORDER = ["sel", "b0", "b1", "meta", "lst0", "c0", "c1", "ident", "lst1", "d0", "e0", "d1"]
ORDER += ["asm", "coefs", "mask", "e1", "roott", "f0", "rrhs", "f1", "g0", "g1", "h0", "i0", "h1", "i1", "j0", "asmt"]
ORDER += ["j1", "k0", "l0", "k1", "l1", "ls0", "m0", "ls1", "m1", "n0", "n1", "invt", "o0", "p0", "o1", "q0", "p1"]
ORDER += ["r0", "q1", "s0", "r1", "s1", "S0", "S1", "t0", "t1", "T0", "T1", "u0", "u1"]
TREE = True
RST = False
ZH = False
OUT = pltpu.VMEM


def nn(a, b):
    return jnp.dot(a, b, preferred_element_type=F32)


def nt(a, b):
    return lax.dot_general(a, b, (((1,), (1,)), ((), ())), preferred_element_type=F32)


def body(dims, *refs):
    T, Z, Y, CR, CC, U, RB, RR, R, H = dims
    C = Y * CORES
    Q = T * C
    G = T * Y
    W = R // H
    NS = Q * CAP
    pc, pr, pz, pu = CR // C, RR // Q, RB // Z, CC // Z
    it = iter(refs)
    take = lambda n: [next(it) for _ in range(n)]
    inv_h, low_h, root_h, rhs_h, rrhs_h = take(5)
    small_h = take(8)
    out_c, out_r = take(2)
    inv, invt, low, lst, ls, sel, root, roott, asm, asmt, ident, rhs, rrhs = take(13)
    slot, msend, mrecv, cfa, cfb, rfa, rfb, scaled = take(8)
    s1, r1, s2, r2, sol, s3, r3, s4, r4, upd = take(10)
    s6, r6, s6b, r6b, rsc, s8, r8, rs, s10, r10 = take(10)
    s11, r11, s11b, r11b, res, s13, r13, mid, cs = take(9)
    small = take(8)
    cdiag, coff, cpat, rdiag, roff, rpat, cmap, piv = small
    in_sem, small_sem, snd, rcv, ysem, zsem, msem = take(7)

    t = lax.axis_index("team")
    r = lax.axis_index("row")
    c = lax.axis_index("col")
    y = c // CORES
    k = c % CORES
    me = t * C + c
    sib = (t, r, y * CORES + (1 - k))

    def plane_id(q):
        return (t * 0 + q // C, r, q % C)

    def z_id(d):
        return (t, (r + d) % Z, c)

    def y_id(d):
        return (t, r, ((y + d) % Y) * CORES + k)

    def g_id(g):
        return (g // Y, r, (g % Y) * CORES + k)

    barrier = pltpu.get_barrier_semaphore()

    def greet_plane(d, carry):
        pl.semaphore_signal(barrier, inc=1, device_id=plane_id((me + d) % Q), device_id_type=MESH)
        return carry

    def greet_z(d, carry):
        pl.semaphore_signal(barrier, inc=1, device_id=z_id(d), device_id_type=MESH)
        return carry

    loads = [pltpu.make_async_copy(rhs_h, rhs, in_sem.at[0])]
    for kk in range(CORES):
        loads.append(pltpu.make_async_copy(inv_h.at[:, kk], inv.at[pl.ds(kk * Y, Y)], in_sem.at[1 + kk]))
    for kk in range(CORES):
        loads.append(pltpu.make_async_copy(low_h.at[:, kk], low.at[pl.ds(kk * Y, Y)], in_sem.at[3 + kk]))
    for kk in range(CORES):
        loads.append(pltpu.make_async_copy(root_h.at[:, kk], root.at[pl.ds(kk * G, G)], in_sem.at[5 + kk]))
    loads.append(pltpu.make_async_copy(rrhs_h, rrhs, in_sem.at[7]))
    small_loads = [pltpu.make_async_copy(a, b, small_sem.at[n]) for n, (a, b) in enumerate(zip(small_h, small))]
    small_loads[6].start()
    for ld in loads[:3]:
        ld.start()
    lax.fori_loop(1, Q, greet_plane, 0)
    lax.fori_loop(1, Z, greet_z, 0)
    for ld in small_loads[7:] + loads[3:] + small_loads[:6]:
        ld.start()

    def send(src, dst, sem_s, sem_r, dev):
        pltpu.make_async_remote_copy(
            src_ref=src, dst_ref=dst, send_sem=sem_s, recv_sem=sem_r, device_id=dev, device_id_type=MESH
        ).start()

    def arrive(view, sem):
        pltpu.make_async_copy(view, view, sem).wait()

    pending = []

    def sent(view, sem):
        pending.append((view, sem))

    def cols(h):
        return pl.ds(h * W, W)

    def halves(n, fn, push):
        def step(i, carry):
            fn(pl.multiple_of(((1 - k) * (n // 2 // MT) + i) % (n // MT) * MT, MT))

            @pl.when(i == n // 2 // MT - 1)
            def _():
                push()

            return carry

        lax.fori_loop(0, n // MT, step, 0)

    def tiled(n, fn, tile=MT):
        def step(i, carry):
            fn(pl.multiple_of(i * tile, tile))
            return carry

        lax.fori_loop(0, n // tile, step, 0)

    def mask_child():
        @pl.when(c > r)
        def _():
            def step(p, carry):
                inv[p] = jnp.zeros((pc, CC), BF)
                return carry

            lax.fori_loop(0, C, step, 0)

        @pl.when(c == r)
        def _():
            rows = lax.broadcasted_iota(jnp.int32, (pc, pc), 0)
            colid = lax.broadcasted_iota(jnp.int32, (pc, pc), 1)
            for p in range(C):
                at = ((p % Y) * CORES + p // Y) * pc
                blk = inv[p, :, at : at + pc].astype(F32)
                blk = jnp.where(colid < rows, blk, jnp.where(colid == rows, 1.0, 0.0))
                inv[p, :, at : at + pc] = blk.astype(BF)
                if at + pc < CC:
                    inv[p, :, at + pc :] = jnp.zeros((pc, CC - at - pc), BF)

    def mask_root():
        for kk in range(2):
            loads[5 + kk].wait()

        @pl.when(me * RB + RB > r * RR)
        def _():
            def step(p, carry):
                g = p % G
                piece = (g // Y) * C + (g % Y) * CORES + p // G
                rows = r * RR + piece * pr + lax.broadcasted_iota(jnp.int32, (pr, RB), 0)
                colid = me * RB + lax.broadcasted_iota(jnp.int32, (pr, RB), 1)
                blk = root[p].astype(F32)
                blk = jnp.where(colid < rows, blk, jnp.where(colid == rows, 1.0, 0.0))
                root[p] = blk.astype(BF)
                return carry

            lax.fori_loop(0, 2 * G, step, 0)

    def make_ident():
        a = lax.broadcasted_iota(jnp.int32, (TILE, TILE), 0)
        b = lax.broadcasted_iota(jnp.int32, (TILE, TILE), 1)
        ident[...] = jnp.where(a == b, 1.0, 0.0).astype(BF)

    def transpose_into(x, xt, m, n, per):
        mt = min(512, m)
        for j in range(n // TILE):

            def step(i, carry):
                blk = x[pl.ds(i * (mt // per), mt // per), :, pl.ds(j * TILE, TILE)].reshape(mt, TILE)
                xt[pl.ds(j * TILE, TILE), pl.ds(pl.multiple_of(i * mt, mt), mt)] = nt(ident[...], blk).astype(BF)
                return carry

            lax.fori_loop(0, m // mt, step, 0)

    def make_slots():
        a = lax.broadcasted_iota(jnp.int32, (128, 128), 0)
        b = lax.broadcasted_iota(jnp.int32, (128, 128), 1)
        tri = jnp.where(a <= b, 1.0, 0.0).astype(BF)
        own_id = lax.broadcasted_iota(jnp.int32, (Q, 128), 0)
        base = jnp.zeros((Q, 1), F32)
        for i in range(U // 128):
            m = jnp.broadcast_to(cmap[:, i * 128 : (i + 1) * 128], (Q, 128))
            owner = m // RB
            hot = jnp.where(owner == own_id, 1.0, 0.0)
            count = nn(hot.astype(BF), tri)
            rank = jnp.sum(hot * (count + base - 1.0), axis=0, keepdims=True)
            base = base + jnp.sum(hot, axis=1, keepdims=True)
            slot[:, i * 128 : (i + 1) * 128] = jnp.broadcast_to(
                owner[0:8] * CAP + rank.astype(jnp.int32), (8, 128)
            )

    def make_sel():
        off = cmap[...] % RB
        row = lax.broadcasted_iota(jnp.int32, (16, U), 0)
        offb = jnp.broadcast_to(off, (16, U))
        probe = jnp.where(row == 0, offb // 16, jnp.where(row == 1, offb % 16, 1))
        probe = jnp.where(row < 3, probe, 0).astype(F32).astype(BF)

        def step(i, carry):
            ids = i * TILE + lax.broadcasted_iota(jnp.int32, (TILE, U), 0)
            blk = jnp.where(ids == slot[0:1, :], 1.0, 0.0).astype(BF)
            sel[pl.ds(pl.multiple_of(i * TILE, TILE), TILE), :] = blk
            info = nt(probe, blk)
            val = jnp.where(info[2:3] > 0.5, info[0:1] * 16.0 + info[1:2], float(RB))
            for j in range(TILE // 128):
                msend[i * (TILE // 128) + j] = jnp.broadcast_to(val[:, j * 128 : (j + 1) * 128], (8, 128))
            return carry

        lax.fori_loop(0, NS // TILE, step, 0)

    def send_meta():
        def step(d, carry):
            q = (me + d) % Q
            send(msend.at[q // 2], mrecv.at[me], msem.at[0], msem.at[1], plane_id(q))
            return carry

        lax.fori_loop(1, Q, step, 0)
        sent(mrecv.at[pl.ds(0, Q - 1)], msem.at[0])
        mrecv[me] = msend[me // 2]

    def make_lst(part_no):
        if part_no == 0:
            for kk in range(2):
                loads[3 + kk].wait()

        def step(i, carry):
            at = pl.ds(pl.multiple_of(i * TILE, TILE), TILE)
            blk = sel[at, :]
            for j in range(CR // 512):
                part = low[pl.ds(j * (512 // pc), 512 // pc)].reshape(512, U)
                lst[at, j * 512 : (j + 1) * 512] = nt(blk, part).astype(BF)
            return carry

        count = NS // TILE // 2
        lax.fori_loop(part_no * count, (part_no + 1) * count, step, 0)

    def make_ls(part_no):
        def step(i, carry):
            part = low[pl.ds(i * (TILE // pc), TILE // pc)].reshape(TILE, U)
            at = pl.ds(pl.multiple_of(i * TILE, TILE), TILE)
            for j in range(NS // 512):
                ls[at, j * 512 : (j + 1) * 512] = nt(part, sel[j * 512 : (j + 1) * 512, :]).astype(BF)
            return carry

        count = CR // TILE // 2
        lax.fori_loop(part_no * count, (part_no + 1) * count, step, 0)

    def make_asm():
        arrive(mrecv.at[pl.ds(0, Q - 1)], msem.at[1])

        def step(j, carry):
            lane = lax.broadcasted_iota(jnp.int32, (8, 128), 1)
            a, b = mrecv[2 * j], mrecv[2 * j + 1]
            ar, br = pltpu.roll(a, 64, 1), pltpu.roll(b, 64, 1)
            first = jnp.where(lane < 64, a, br)
            second = jnp.where(lane < 64, ar, b)
            kf = k.astype(F32)
            val = first * (1.0 - kf) + second * kf
            ids = lax.broadcasted_iota(jnp.int32, (RB, 128), 0).astype(F32)
            blk = jnp.where(ids == val[0:1, :], 1.0, 0.0).astype(BF)
            asm[:, pl.ds(pl.multiple_of(j * 128, 128), 128)] = blk
            return carry

        lax.fori_loop(0, Q // 2, step, 0)

    def make_asmt():
        def step(i, carry):
            at = pl.multiple_of(i * TILE, TILE)
            asmt[pl.ds(at, TILE), :] = nt(ident[...], asm[:, pl.ds(at, TILE)]).astype(BF)
            return carry

        lax.fori_loop(0, NS // TILE, step, 0)

    def coefficients(dref, oref, pref, fa, fb, start, n):
        first = (start // 128) * 128
        lane = lax.broadcasted_iota(jnp.int32, (128, 128), 1)
        even = lane % 2 == 0
        for i in range(max(1, n // 128)):
            at = pl.ds(pl.multiple_of(first + i * 128, 128), 128)
            a = jnp.broadcast_to(dref[:, at], (128, 128))
            o = jnp.broadcast_to(oref[:, at], (128, 128))
            p = jnp.broadcast_to(pref[:, at], (128, 128))
            partner = jnp.where(even, pltpu.roll(a, 127, 1), pltpu.roll(a, 1, 1))
            coup = jnp.where(p == 1, o, 0.0)
            coup = jnp.where(even, coup, pltpu.roll(coup, 1, 1))
            det = a * partner - coup * coup
            fa[pl.ds(i * 128, 128), :] = (partner / det).T
            fb[pl.ds(i * 128, 128), :] = (-coup / det).T

    def pivot(v, fa, fb, start, n):
        at = pl.ds(0, n) if n >= 128 else pl.ds(pl.multiple_of(start % 128, n), n)
        a = jnp.concatenate([fa[at, :]] * (W // 128), axis=1)
        b = jnp.concatenate([fb[at, :]] * (W // 128), axis=1)
        even = lax.broadcasted_iota(jnp.int32, (n, W), 0) % 2 == 0
        partner = jnp.where(even, pltpu.roll(v, n - 1, 0), pltpu.roll(v, 1, 0))
        return a * v + b * partner

    def make_coefs():
        coefficients(cdiag, coff, cpat, cfa, cfb, c * pc, pc)
        coefficients(rdiag, roff, rpat, rfa, rfb, me * pr, pr)

    def away(i, size):
        return size // 2 + (1 - 2 * (i % 2)) * ((i + 1) // 2)

    half = CR // 2

    def col_core_send(h, s_a, r_a, st):
        send(s_a.at[h, pl.ds((1 - k) * half, half)], r_a.at[h], snd.at[h, st], rcv.at[h, st], sib)

    def col_y_send(h, s_a, r_a, s_b, r_b, st):
        arrive(r_a.at[h], rcv.at[h, st])
        s_b[h] = (s_a[h, pl.ds(pl.multiple_of(k * half, half), half), :].astype(F32) + r_a[h].astype(F32)).astype(BF)
        for d in [away(n, Y) for n in range(Y - 1)]:
            p = (y + d) % Y
            send(s_b.at[h, pl.ds(p * pc, pc)], r_b.at[h, pl.ds((d - 1) * pc, pc)], snd.at[h, st + 1], rcv.at[h, st + 1], y_id(d))
        sent(r_b.at[h], snd.at[h, st + 1])

    def col_sum(h, s_b, r_b, st):
        arrive(r_b.at[h], rcv.at[h, st + 1])
        acc = s_b[h, pl.ds(pl.multiple_of(y * pc, pc), pc), :].astype(F32)
        for d in range(Y - 1):
            acc = acc + r_b[h, d * pc : (d + 1) * pc, :].astype(F32)
        return acc

    def col_gather(h, buf, value, st, ys):
        at = pl.ds(pl.multiple_of(k * half + y * pc, pc), pc)
        buf[h, at, :] = value
        for d in [away(n, Y) for n in range(Y - 1)]:
            send(buf.at[h, at], buf.at[h, at], snd.at[h, st], ysem.at[h, ys, d - 1], y_id(d))
        send(buf.at[h, at], buf.at[h, at], snd.at[h, st + 1], rcv.at[h, st + 1], sib)
        sent(buf.at[h, pl.ds(0, (Y - 1) * pc)], snd.at[h, st])
        sent(buf.at[h, pl.ds(0, half)], snd.at[h, st + 1])

    def col_forward(h, buf, st, ys):
        for d in (1, Y - 1, 2) if Y == 4 else range(1, Y):
            at = pl.ds(pl.multiple_of(k * half + ((y + Y - d) % Y) * pc, pc), pc)
            arrive(buf.at[h, at], ysem.at[h, ys, d - 1])
            send(buf.at[h, at], buf.at[h, at], snd.at[h, st + 1], rcv.at[h, st + 1], sib)

    def col_gathered(h, buf, st):
        arrive(buf.at[h, pl.ds(0, half)], rcv.at[h, st + 1])

    def far(i):
        return away(i, Z)

    def chip(n):
        return (t + away(n // Y, T)) % T * Y + (y + away(n % Y, Y)) % Y

    def z_scatter(h, s, rr, n, st):
        def step(i, carry):
            d = far(i)
            to = (r + d) % Z
            send(s.at[h, pl.ds(to * n, n)], rr.at[h, pl.ds((d - 1) * n, n)], snd.at[h, st], rcv.at[h, st], z_id(d))
            return carry

        lax.fori_loop(0, Z - 1, step, 0)
        sent(rr.at[h], snd.at[h, st])

    def z_product(h, mat, vec, s, rr, n, st):
        side = Z // 2
        rows = side * n

        def step(i, carry):
            g = (r // side + 1 + i) % 2
            at = pl.multiple_of(g * rows, rows)
            s[h, pl.ds(at, rows), :] = nn(mat[pl.ds(at, rows), :], vec[h]).astype(BF)
            for j in range(side):
                to = g * side + j

                @pl.when(to != r)
                def _():
                    d = (to - r + Z) % Z
                    send(s.at[h, pl.ds(to * n, n)], rr.at[h, pl.ds((d - 1) * n, n)], snd.at[h, st], rcv.at[h, st], (t, to, c))

            return carry

        lax.fori_loop(0, 2, step, 0)
        sent(rr.at[h], snd.at[h, st])

    def z_sum(h, s, rr, n, st):
        arrive(rr.at[h], rcv.at[h, st])
        acc = s[h, pl.ds(pl.multiple_of(r * n, n), n), :].astype(F32)
        for d in range(Z - 1):
            acc = acc + rr[h, d * n : (d + 1) * n, :].astype(F32)
        return acc

    def z_gather(h, buf, value, n, st):
        at = pl.ds(pl.multiple_of(r * n, n), n)
        buf[h, at, :] = value

        def step(i, carry):
            send(buf.at[h, at], buf.at[h, at], snd.at[h, st], rcv.at[h, st], z_id(far(i)))
            return carry

        lax.fori_loop(0, Z - 1, step, 0)
        sent(buf.at[h, pl.ds(0, (Z - 1) * n)], snd.at[h, st])

    def z_gathered(h, buf, n, st):
        arrive(buf.at[h, pl.ds(0, (Z - 1) * n)], rcv.at[h, st])

    def z_tree_scatter(h, s, mid, rr, n, st):
        def part(to):
            return s.at[h, pl.ds(((r + to) % Z) * n, n)]

        for i, (to, via) in enumerate(((3, 1), (Z - 3, Z - 1), (4, (2, Z - 2)[h % 2]))):
            sem = zsem.at[h, 2 + (i if i < 2 else h % 2)]
            send(part(to), mid.at[h, pl.ds(i * n, n)], snd.at[h, st], sem, z_id(via))
        for i, to in enumerate((1, Z - 1)):
            send(part(to), rr.at[h, pl.ds(i * n, n)], snd.at[h, st], rcv.at[h, st], z_id(to))
        sent(s.at[h, pl.ds(0, 5 * n)], snd.at[h, st])

    def z_tree_pass(h, s, mid, rr, n, st):
        for i, to in enumerate((2, Z - 2)):
            both = i == h % 2
            view = mid.at[h, pl.ds(0, (2 if both else 1) * n)]
            arrive(view, zsem.at[h, 2 + i])
            at = pl.ds(pl.multiple_of(((r + to) % Z) * n, n), n)
            acc = s[h, at, :].astype(F32) + mid[h, i * n : (i + 1) * n, :].astype(F32)
            if both:
                acc = acc + mid[h, 2 * n : 3 * n, :].astype(F32)
            s[h, at, :] = acc.astype(BF)
            send(s.at[h, at], rr.at[h, pl.ds((2 + i) * n, n)], snd.at[h, st + 1], rcv.at[h, st], z_id(to))
        sent(s.at[h, pl.ds(0, 2 * n)], snd.at[h, st + 1])

    def z_tree_sum(h, s, rr, n, st):
        arrive(rr.at[h, pl.ds(0, 4 * n)], rcv.at[h, st])
        acc = s[h, pl.ds(pl.multiple_of(r * n, n), n), :].astype(F32)
        for d in range(4):
            acc = acc + rr[h, d * n : (d + 1) * n, :].astype(F32)
        return acc

    def z_tree(h, buf, value, n, st):
        at = pl.ds(pl.multiple_of(r * n, n), n)
        buf[h, at, :] = value
        for i, d in enumerate((2, Z - 2)):
            send(buf.at[h, at], buf.at[h, at], snd.at[h, st], zsem.at[h, i], z_id(d))
        for d in (1, Z - 1):
            send(buf.at[h, at], buf.at[h, at], snd.at[h, st], rcv.at[h, st], z_id(d))
        sent(buf.at[h, pl.ds(0, (Z - 1) * n)], snd.at[h, st])

    def z_tree_forward(h, buf, n, st):
        for i, d in enumerate((2, Z - 2)):
            at = pl.ds(pl.multiple_of(((r + Z - d) % Z) * n, n), n)
            arrive(buf.at[h, at], zsem.at[h, i])
            if i == h % 2:
                send(buf.at[h, at], buf.at[h, at], snd.at[h, st], rcv.at[h, st], z_id(d))
            send(buf.at[h, at], buf.at[h, at], snd.at[h, st], rcv.at[h, st], z_id((1, Z - 1)[i]))

    def exchange(h, mat, vec, s, rr, st):
        per = XT // CAP
        groups = NS // XT

        def step(i, carry):
            g = (me // per + 1 + i) % groups
            at = pl.multiple_of(g * XT, XT)
            s[h, pl.ds(at, XT), :] = nn(mat[pl.ds(at, XT), :], vec[h]).astype(BF)
            for j in range(per):
                q = g * per + j

                @pl.when(q != me)
                def _():
                    send(s.at[h, pl.ds(q * CAP, CAP)], rr.at[h, pl.ds(me * CAP, CAP)], snd.at[h, st], rcv.at[h, st], plane_id(q))

            return carry

        lax.fori_loop(0, groups, step, 0)
        sent(rr.at[h, pl.ds(0, NS - CAP)], snd.at[h, st])
        at = pl.ds(pl.multiple_of(me * CAP, CAP), CAP)
        rr[h, at, :] = s[h, at, :]

    def exchanged(h, rr, st):
        arrive(rr.at[h, pl.ds(0, NS - CAP)], rcv.at[h, st])

    def live(h):
        rows = r * CR + c * pc + lax.broadcasted_iota(jnp.int32, (pc, W), 0)
        return rows < piv[...]

    def b(h):
        col_y_send(h, s1, r1, s2, r2, 0)

    def cc(h):
        acc = col_sum(h, s2, r2, 0)
        solved = jnp.where(live(h), acc, 0.0).astype(BF)
        col_gather(h, sol, solved, 2, 0)

    def d(h):
        col_forward(h, sol, 2, 0)

    def e(h):
        col_gathered(h, sol, 2)
        exchange(h, lst, sol, s3, r3, 4)

    def f(h):
        exchanged(h, r3, 4)
        if ZH:
            z_product(h, asm, r3, s4, r4, pz, 5)
            return

        def fn(i):
            s4[h, pl.ds(i, MT), :] = nn(asm[pl.ds(i, MT), :], r3[h]).astype(BF)

        tiled(RB, fn)
        z_scatter(h, s4, r4, pz, 5)

    def g(h):
        acc = z_sum(h, s4, r4, pz, 5)
        mine = rrhs[pl.ds(pl.multiple_of(r * pz, pz), pz), h * W : (h + 1) * W].astype(F32)
        z_gather(h, upd, (mine - acc).astype(BF), pz, 6)

    def hh(h):
        z_gathered(h, upd, pz, 6)

        def fn(i):
            tile = root[pl.ds(i // pr, MT // pr)].reshape(MT, RB)
            s6[h, pl.ds(i, MT), :] = nn(tile, upd[h]).astype(BF)

        rh = RR // 2
        halves(RR, fn, lambda: send(s6.at[h, pl.ds((1 - k) * rh, rh)], r6.at[h], snd.at[h, 7], rcv.at[h, 7], sib))
        sent(r6.at[h], snd.at[h, 7])

    def i_(h):
        arrive(r6.at[h], rcv.at[h, 7])
        rh = RR // 2
        gi = t * Y + y

        def step(j, carry):
            p = chip(j)
            at = pl.ds(pl.multiple_of(p * pr, pr), pr)
            mine = pl.ds(pl.multiple_of(k * rh + p * pr, pr), pr)
            s6b[h, at, :] = (s6[h, mine, :].astype(F32) + r6[h, at, :].astype(F32)).astype(BF)

            @pl.when(p != gi)
            def _():
                send(s6b.at[h, at], r6b.at[h, pl.ds(j * pr, pr)], snd.at[h, 8], rcv.at[h, 8], g_id(p))

            return carry

        lax.fori_loop(0, G, step, 0)
        sent(r6b.at[h], snd.at[h, 8])

    def j_(h):
        arrive(r6b.at[h], rcv.at[h, 8])
        gi = t * Y + y
        acc = s6b[h, pl.ds(pl.multiple_of(gi * pr, pr), pr), :].astype(F32)
        for n in range(G - 1):
            acc = acc + r6b[h, n * pr : (n + 1) * pr, :].astype(F32)
        value = pivot(acc, rfa, rfb, me * pr, pr).astype(BF)
        at = pl.ds(pl.multiple_of((k * G + gi) * pr, pr), pr)
        rsc[h, at, :] = value

        def step(n, carry):
            send(rsc.at[h, at], rsc.at[h, at], snd.at[h, 9], rcv.at[h, 9], g_id(chip(n - 1)))
            return carry

        lax.fori_loop(1, G, step, 0)
        sent(rsc.at[h, pl.ds(0, (G - 1) * pr)], snd.at[h, 9])

    def k_(h):
        rh = RR // 2
        arrive(rsc.at[h, pl.ds(0, (G - 1) * pr)], rcv.at[h, 9])
        mine = pl.ds(k * rh, rh)
        send(rsc.at[h, mine], rsc.at[h, mine], snd.at[h, 10], rcv.at[h, 10], sib)
        sent(rsc.at[h, pl.ds(0, rh)], snd.at[h, 10])

    def l_(h):
        arrive(rsc.at[h, pl.ds(0, RR // 2)], rcv.at[h, 10])
        if ZH:
            z_product(h, roott, rsc, s8, r8, pz, 11)
            return

        def fn(i):
            s8[h, pl.ds(i, MT), :] = nn(roott[pl.ds(i, MT), :], rsc[h]).astype(BF)

        tiled(RB, fn)
        z_scatter(h, s8, r8, pz, 11)

    def m_(h):
        z_gather(h, rs, z_sum(h, s8, r8, pz, 11).astype(BF), pz, 12)

    def n_(h):
        z_gathered(h, rs, pz, 12)
        exchange(h, asmt, rs, s10, r10, 13)
        out_r[:, h * W : (h + 1) * W] = rs[h].astype(F32)

    def o_(h):
        exchanged(h, r10, 13)

        def fn(i):
            s11[h, pl.ds(i, MT), :] = nn(ls[pl.ds(i, MT), :], r10[h]).astype(BF)

        halves(CR, fn, lambda: col_core_send(h, s11, r11, 14))
        sent(r11.at[h], snd.at[h, 14])

    def p_(h):
        col_y_send(h, s11, r11, s11b, r11b, 14)

    def q_(h):
        acc = col_sum(h, s11b, r11b, 14)
        value = jnp.where(live(h), scaled[h] - acc, 0.0).astype(BF)
        col_gather(h, res, value, 16, 1)

    def r_(h):
        col_forward(h, res, 16, 1)

    def s_(h):
        col_gathered(h, res, 16)
        if ZH:
            z_product(h, invt, res, s13, r13, pu, 18)
            return

        def fn(i):
            s13[h, pl.ds(i, MT), :] = nn(invt[pl.ds(i, MT), :], res[h]).astype(BF)

        tiled(CC, fn)
        if RST:
            z_tree_scatter(h, s13, mid, r13, pu, 18)
        else:
            z_scatter(h, s13, r13, pu, 18)

    def s2_(h):
        if RST:
            z_tree_pass(h, s13, mid, r13, pu, 18)

    def t_(h):
        gather = z_tree if TREE else z_gather
        gather(h, cs, (z_tree_sum if RST else z_sum)(h, s13, r13, pu, 18).astype(BF), pu, 20)

    def t2_(h):
        if TREE:
            z_tree_forward(h, cs, pu, 20)

    def u_(h):
        arrive(cs.at[h, pl.ds(0, (Z - 3 if TREE else Z - 1) * pu)], rcv.at[h, 20])
        out_c[:, h * W : (h + 1) * W] = cs[h].astype(F32)

    def first(start):
        def fn(i):
            at = pl.multiple_of(start + i, MT)
            value = nn(inv[pl.ds(at // pc, MT // pc)].reshape(MT, CC), rhs[...]).astype(BF)
            for h in range(H):
                s1[h, pl.ds(at, MT), :] = value[:, h * W : (h + 1) * W]

        tiled(half, fn)

    def coefs():
        for n in range(6):
            small_loads[n].wait()
        make_coefs()
        at = pl.ds(pl.multiple_of(k * half + y * pc, pc), pc)
        for h in range(H):
            scaled[h] = pivot(sol[h, at, :].astype(F32), cfa, cfb, c * pc, pc)

    small_loads[6].wait()
    make_slots()
    for n in range(3):
        loads[n].wait()
    mask_child()
    first((1 - k) * half)
    small_loads[7].wait()
    pl.semaphore_wait(barrier, Q - 1 + Z - 1)
    for h in range(H):
        col_core_send(h, s1, r1, 0)
        sent(r1.at[h], snd.at[h, 0])
    first(k * half)
    local = {
        "sel": make_sel,
        "meta": send_meta,
        "lst0": lambda: make_lst(0),
        "lst1": lambda: make_lst(1),
        "ident": make_ident,
        "asm": make_asm,
        "coefs": coefs,
        "mask": mask_root,
        "roott": lambda: transpose_into(root, roott, RR, RB, pr),
        "ls0": lambda: make_ls(0),
        "ls1": lambda: make_ls(1),
        "asmt": make_asmt,
        "invt": lambda: transpose_into(inv, invt, CR, CC, pc),
        "rrhs": loads[7].wait,
    }
    steps = [b, cc, d, e, f, g, hh, i_, j_, k_, l_, m_, n_, o_, p_, q_, r_, s_, s2_, t_, t2_, u_]
    names = dict(zip("bcdefghijklmnopqrsStTu", steps))
    for item in ORDER:
        if item in local:
            local[item]()
        else:
            names[item[0]](int(item[1]))
    for view, sem in pending:
        arrive(view, sem)


def shards(dims, *args):
    (child_inverse, child_lower, child_rhs, child_diag, child_off, child_pattern, child_pivots, child_map,
     root_inverse, root_rhs, root_diag, root_off, root_pattern) = args
    T, Z, Y, CR, CC, U, RB, RR, R, H = dims
    C, Q, G, W = Y * CORES, T * Y * CORES, T * Y, R // H
    NS = Q * CAP
    pc, pr, pz, pu = CR // C, RR // Q, RB // Z, CC // Z

    def chain(rows):
        return pltpu.VMEM((H, rows, W), BF)

    vm = lambda *shape: pltpu.VMEM(shape, BF)
    fm = lambda *shape: pltpu.VMEM(shape, F32)
    half = CR // 2
    scratch = [
        vm(C, pc, CC), vm(CC, CR), vm(C, pc, U), vm(NS, CR), vm(CR, NS), vm(NS, U), vm(Q, pr, RB), vm(RB, RR),
        vm(RB, NS), vm(NS, RB), vm(TILE, TILE), vm(CC, R), vm(RB, R),
        pltpu.VMEM((8, U), jnp.int32), fm(Q // 2, 8, 128), fm(Q, 8, 128),
        fm(max(pc, 128), 128), fm(max(pc, 128), 128), fm(max(pr, 128), 128), fm(max(pr, 128), 128), fm(H, pc, W),
        chain(CR), chain(half), chain(half), chain((Y - 1) * pc), chain(CR), chain(NS), chain(NS), chain(RB),
        chain((Z - 1) * pz), chain(RB),
        chain(RR), chain(RR // 2), chain(RR // 2), chain((G - 1) * pr), chain(RR), chain(RB), chain((Z - 1) * pz),
        chain(RB), chain(NS), chain(NS),
        chain(CR), chain(half), chain(half), chain((Y - 1) * pc), chain(CR), chain(CC), chain((Z - 1) * pu), chain(3 * pu), chain(CC),
        *[pltpu.VMEM((1, n), dt) for n, dt in ((CR, F32), (CR, F32), (CR, jnp.int32), (RR, F32), (RR, F32), (RR, jnp.int32), (U, jnp.int32), (1, jnp.int32))],
        pltpu.SemaphoreType.DMA((8,)), pltpu.SemaphoreType.DMA((8,)), pltpu.SemaphoreType.DMA((H, 21)), pltpu.SemaphoreType.DMA((H, 21)),
        pltpu.SemaphoreType.DMA((H, 2, Y - 1)), pltpu.SemaphoreType.DMA((H, 4)), pltpu.SemaphoreType.DMA((2,)),
    ]
    anyspec = pl.BlockSpec(memory_space=pl.ANY)
    vspec = pl.BlockSpec(memory_space=pltpu.VMEM)
    flops = 2 * R * (2 * CR * CC + 2 * NS * CR + 2 * RB * NS + 2 * RR * RB)
    child, rooted = pl.pallas_call(
        functools.partial(body, dims),
        name="substitution",
        out_shape=(OUT((CC, R), F32), OUT((RB, R), F32)),
        in_specs=[anyspec] * 13,
        out_specs=(vspec, vspec),
        scratch_shapes=scratch,
        cost_estimate=pl.CostEstimate(flops=flops, bytes_accessed=8 << 20, transcendentals=0),
        compiler_params=pltpu.CompilerParams(collective_id=0, has_side_effects=True, vmem_limit_bytes=58 << 20),
    )(
        child_inverse.reshape(Y, CORES, pc, CC),
        child_lower.reshape(Y, CORES, pc, U),
        root_inverse.reshape(G, CORES, pr, RB),
        child_rhs.reshape(CC, R),
        root_rhs,
        child_diag.reshape(1, CR),
        child_off.reshape(1, CR),
        child_pattern.reshape(1, CR),
        root_diag.reshape(1, RR),
        root_off.reshape(1, RR),
        root_pattern.reshape(1, RR),
        child_map.reshape(1, U),
        child_pivots.reshape(1, 1),
    )
    return (child[None], rooted)


def solution(mesh):
    T, Z, C = mesh.shape["team"], mesh.shape["row"], mesh.shape["col"]

    def run(*args):
        pc_, uc = args[0].shape[1], args[1].shape[2]
        fr, R = args[9].shape
        dims = (T, Z, C // CORES, pc_ // Z, pc_ // C, uc // C, fr // (T * C), fr // Z, R, CHAINS)
        return jax.shard_map(
            functools.partial(shards, dims),
            mesh=mesh,
            in_specs=(
                P("team", "row", "col"),
                P("team", "row", "col"),
                P("team", "col", None),
                P("team", "row"),
                P("team", "row"),
                P("team", "row"),
                P("team"),
                P("team", "col"),
                P("row", ("team", "col")),
                P(("team", "col"), None),
                P("row"),
                P("row"),
                P("row"),
            ),
            out_specs=(P("team", "col", None), P(("team", "col"), None)),
            check_vma=False,
        )(*args)

    return run
```

```python
import functools

import jax
import jax.numpy as jnp
from jax import lax
from jax.experimental import pallas as pl
from jax.experimental.pallas import tpu as pltpu
from jax.sharding import PartitionSpec as P

BF = jnp.bfloat16
F32 = jnp.float32
MESH = pl.DeviceIdType.MESH
CORES = 2
CAP = 64
TILE = 256
MT = 512
XT = 256
CHAINS = 2
ORDER = ["sel", "b0", "b1", "meta", "lst0", "c0", "c1", "ident", "lst1", "d0", "e0", "d1"]
ORDER += ["asm", "coefs", "mask", "e1", "roott", "f0", "rrhs", "f1", "g0", "g1", "h0", "i0", "h1", "i1", "j0", "asmt"]
ORDER += ["j1", "k0", "l0", "k1", "l1", "ls0", "m0", "ls1", "m1", "n0", "n1", "invt", "o0", "p0", "o1", "q0", "p1"]
ORDER += ["r0", "q1", "s0", "r1", "s1", "S0", "S1", "t0", "t1", "T0", "T1", "u0", "u1"]
TREE = True
RST = False
ZH = False
OUT = pltpu.VMEM


def nn(a, b):
    return jnp.dot(a, b, preferred_element_type=F32)


def nt(a, b):
    return lax.dot_general(a, b, (((1,), (1,)), ((), ())), preferred_element_type=F32)


def body(dims, *refs):
    T, Z, Y, CR, CC, U, RB, RR, R, H = dims
    C = Y * CORES
    Q = T * C
    G = T * Y
    W = R // H
    NS = Q * CAP
    pc, pr, pz, pu = CR // C, RR // Q, RB // Z, CC // Z
    it = iter(refs)
    take = lambda n: [next(it) for _ in range(n)]
    inv_h, low_h, root_h, rhs_h, rrhs_h = take(5)
    small_h = take(8)
    out_c, out_r = take(2)
    inv, invt, low, lst, ls, sel, root, roott, asm, asmt, ident, rhs, rrhs = take(13)
    slot, msend, mrecv, cfa, cfb, rfa, rfb, scaled = take(8)
    s1, r1, s2, r2, sol, s3, r3, s4, r4, upd = take(10)
    s6, r6, s6b, r6b, rsc, s8, r8, rs, s10, r10 = take(10)
    s11, r11, s11b, r11b, res, s13, r13, mid, cs = take(9)
    small = take(8)
    cdiag, coff, cpat, rdiag, roff, rpat, cmap, piv = small
    in_sem, small_sem, snd, rcv, ysem, zsem, msem = take(7)

    t = lax.axis_index("team")
    r = lax.axis_index("row")
    c = lax.axis_index("col")
    y = c // CORES
    k = c % CORES
    me = t * C + c
    sib = (t, r, y * CORES + (1 - k))

    def plane_id(q):
        return (t * 0 + q // C, r, q % C)

    def z_id(d):
        return (t, (r + d) % Z, c)

    def y_id(d):
        return (t, r, ((y + d) % Y) * CORES + k)

    def g_id(g):
        return (g // Y, r, (g % Y) * CORES + k)

    barrier = pltpu.get_barrier_semaphore()

    def greet_plane(d, carry):
        pl.semaphore_signal(barrier, inc=1, device_id=plane_id((me + d) % Q), device_id_type=MESH)
        return carry

    def greet_z(d, carry):
        pl.semaphore_signal(barrier, inc=1, device_id=z_id(d), device_id_type=MESH)
        return carry

    loads = [pltpu.make_async_copy(rhs_h, rhs, in_sem.at[0])]
    for kk in range(CORES):
        loads.append(pltpu.make_async_copy(inv_h.at[:, kk], inv.at[pl.ds(kk * Y, Y)], in_sem.at[1 + kk]))
    for kk in range(CORES):
        loads.append(pltpu.make_async_copy(low_h.at[:, kk], low.at[pl.ds(kk * Y, Y)], in_sem.at[3 + kk]))
    for kk in range(CORES):
        loads.append(pltpu.make_async_copy(root_h.at[:, kk], root.at[pl.ds(kk * G, G)], in_sem.at[5 + kk]))
    loads.append(pltpu.make_async_copy(rrhs_h, rrhs, in_sem.at[7]))
    small_loads = [pltpu.make_async_copy(a, b, small_sem.at[n]) for n, (a, b) in enumerate(zip(small_h, small))]
    small_loads[6].start()
    for ld in loads[:3]:
        ld.start()
    lax.fori_loop(1, Q, greet_plane, 0)
    lax.fori_loop(1, Z, greet_z, 0)
    for ld in small_loads[7:] + loads[3:] + small_loads[:6]:
        ld.start()

    def send(src, dst, sem_s, sem_r, dev):
        pltpu.make_async_remote_copy(
            src_ref=src, dst_ref=dst, send_sem=sem_s, recv_sem=sem_r, device_id=dev, device_id_type=MESH
        ).start()

    def arrive(view, sem):
        pltpu.make_async_copy(view, view, sem).wait()

    pending = []

    def sent(view, sem):
        pending.append((view, sem))

    def cols(h):
        return pl.ds(h * W, W)

    def halves(n, fn, push):
        def step(i, carry):
            fn(pl.multiple_of(((1 - k) * (n // 2 // MT) + i) % (n // MT) * MT, MT))

            @pl.when(i == n // 2 // MT - 1)
            def _():
                push()

            return carry

        lax.fori_loop(0, n // MT, step, 0)

    def tiled(n, fn, tile=MT):
        def step(i, carry):
            fn(pl.multiple_of(i * tile, tile))
            return carry

        lax.fori_loop(0, n // tile, step, 0)

    def mask_child():
        @pl.when(c > r)
        def _():
            def step(p, carry):
                inv[p] = jnp.zeros((pc, CC), BF)
                return carry

            lax.fori_loop(0, C, step, 0)

        @pl.when(c == r)
        def _():
            rows = lax.broadcasted_iota(jnp.int32, (pc, pc), 0)
            colid = lax.broadcasted_iota(jnp.int32, (pc, pc), 1)
            for p in range(C):
                at = ((p % Y) * CORES + p // Y) * pc
                blk = inv[p, :, at : at + pc].astype(F32)
                blk = jnp.where(colid < rows, blk, jnp.where(colid == rows, 1.0, 0.0))
                inv[p, :, at : at + pc] = blk.astype(BF)
                if at + pc < CC:
                    inv[p, :, at + pc :] = jnp.zeros((pc, CC - at - pc), BF)

    def mask_root():
        for kk in range(2):
            loads[5 + kk].wait()

        @pl.when(me * RB + RB > r * RR)
        def _():
            def step(p, carry):
                g = p % G
                piece = (g // Y) * C + (g % Y) * CORES + p // G
                rows = r * RR + piece * pr + lax.broadcasted_iota(jnp.int32, (pr, RB), 0)
                colid = me * RB + lax.broadcasted_iota(jnp.int32, (pr, RB), 1)
                blk = root[p].astype(F32)
                blk = jnp.where(colid < rows, blk, jnp.where(colid == rows, 1.0, 0.0))
                root[p] = blk.astype(BF)
                return carry

            lax.fori_loop(0, 2 * G, step, 0)

    def make_ident():
        a = lax.broadcasted_iota(jnp.int32, (TILE, TILE), 0)
        b = lax.broadcasted_iota(jnp.int32, (TILE, TILE), 1)
        ident[...] = jnp.where(a == b, 1.0, 0.0).astype(BF)

    def transpose_into(x, xt, m, n, per):
        mt = min(512, m)
        for j in range(n // TILE):

            def step(i, carry):
                blk = x[pl.ds(i * (mt // per), mt // per), :, pl.ds(j * TILE, TILE)].reshape(mt, TILE)
                xt[pl.ds(j * TILE, TILE), pl.ds(pl.multiple_of(i * mt, mt), mt)] = nt(ident[...], blk).astype(BF)
                return carry

            lax.fori_loop(0, m // mt, step, 0)

    def make_slots():
        a = lax.broadcasted_iota(jnp.int32, (128, 128), 0)
        b = lax.broadcasted_iota(jnp.int32, (128, 128), 1)
        tri = jnp.where(a <= b, 1.0, 0.0).astype(BF)
        own_id = lax.broadcasted_iota(jnp.int32, (Q, 128), 0)
        base = jnp.zeros((Q, 1), F32)
        for i in range(U // 128):
            m = jnp.broadcast_to(cmap[:, i * 128 : (i + 1) * 128], (Q, 128))
            owner = m // RB
            hot = jnp.where(owner == own_id, 1.0, 0.0)
            count = nn(hot.astype(BF), tri)
            rank = jnp.sum(hot * (count + base - 1.0), axis=0, keepdims=True)
            base = base + jnp.sum(hot, axis=1, keepdims=True)
            slot[:, i * 128 : (i + 1) * 128] = jnp.broadcast_to(
                owner[0:8] * CAP + rank.astype(jnp.int32), (8, 128)
            )

    def make_sel():
        off = cmap[...] % RB
        row = lax.broadcasted_iota(jnp.int32, (16, U), 0)
        offb = jnp.broadcast_to(off, (16, U))
        probe = jnp.where(row == 0, offb // 16, jnp.where(row == 1, offb % 16, 1))
        probe = jnp.where(row < 3, probe, 0).astype(F32).astype(BF)

        def step(i, carry):
            ids = i * TILE + lax.broadcasted_iota(jnp.int32, (TILE, U), 0)
            blk = jnp.where(ids == slot[0:1, :], 1.0, 0.0).astype(BF)
            sel[pl.ds(pl.multiple_of(i * TILE, TILE), TILE), :] = blk
            info = nt(probe, blk)
            val = jnp.where(info[2:3] > 0.5, info[0:1] * 16.0 + info[1:2], float(RB))
            for j in range(TILE // 128):
                msend[i * (TILE // 128) + j] = jnp.broadcast_to(val[:, j * 128 : (j + 1) * 128], (8, 128))
            return carry

        lax.fori_loop(0, NS // TILE, step, 0)

    def send_meta():
        def step(d, carry):
            q = (me + d) % Q
            send(msend.at[q // 2], mrecv.at[me], msem.at[0], msem.at[1], plane_id(q))
            return carry

        lax.fori_loop(1, Q, step, 0)
        sent(mrecv.at[pl.ds(0, Q - 1)], msem.at[0])
        mrecv[me] = msend[me // 2]

    def make_lst(part_no):
        if part_no == 0:
            for kk in range(2):
                loads[3 + kk].wait()

        def step(i, carry):
            at = pl.ds(pl.multiple_of(i * TILE, TILE), TILE)
            blk = sel[at, :]
            for j in range(CR // 512):
                part = low[pl.ds(j * (512 // pc), 512 // pc)].reshape(512, U)
                lst[at, j * 512 : (j + 1) * 512] = nt(blk, part).astype(BF)
            return carry

        count = NS // TILE // 2
        lax.fori_loop(part_no * count, (part_no + 1) * count, step, 0)

    def make_ls(part_no):
        def step(i, carry):
            part = low[pl.ds(i * (TILE // pc), TILE // pc)].reshape(TILE, U)
            at = pl.ds(pl.multiple_of(i * TILE, TILE), TILE)
            for j in range(NS // 512):
                ls[at, j * 512 : (j + 1) * 512] = nt(part, sel[j * 512 : (j + 1) * 512, :]).astype(BF)
            return carry

        count = CR // TILE // 2
        lax.fori_loop(part_no * count, (part_no + 1) * count, step, 0)

    def make_asm():
        arrive(mrecv.at[pl.ds(0, Q - 1)], msem.at[1])

        def step(j, carry):
            lane = lax.broadcasted_iota(jnp.int32, (8, 128), 1)
            a, b = mrecv[2 * j], mrecv[2 * j + 1]
            ar, br = pltpu.roll(a, 64, 1), pltpu.roll(b, 64, 1)
            first = jnp.where(lane < 64, a, br)
            second = jnp.where(lane < 64, ar, b)
            kf = k.astype(F32)
            val = first * (1.0 - kf) + second * kf
            ids = lax.broadcasted_iota(jnp.int32, (RB, 128), 0).astype(F32)
            blk = jnp.where(ids == val[0:1, :], 1.0, 0.0).astype(BF)
            asm[:, pl.ds(pl.multiple_of(j * 128, 128), 128)] = blk
            return carry

        lax.fori_loop(0, Q // 2, step, 0)

    def make_asmt():
        def step(i, carry):
            at = pl.multiple_of(i * TILE, TILE)
            asmt[pl.ds(at, TILE), :] = nt(ident[...], asm[:, pl.ds(at, TILE)]).astype(BF)
            return carry

        lax.fori_loop(0, NS // TILE, step, 0)

    def coefficients(dref, oref, pref, fa, fb, start, n):
        first = (start // 128) * 128
        lane = lax.broadcasted_iota(jnp.int32, (128, 128), 1)
        even = lane % 2 == 0
        for i in range(max(1, n // 128)):
            at = pl.ds(pl.multiple_of(first + i * 128, 128), 128)
            a = jnp.broadcast_to(dref[:, at], (128, 128))
            o = jnp.broadcast_to(oref[:, at], (128, 128))
            p = jnp.broadcast_to(pref[:, at], (128, 128))
            partner = jnp.where(even, pltpu.roll(a, 127, 1), pltpu.roll(a, 1, 1))
            coup = jnp.where(p == 1, o, 0.0)
            coup = jnp.where(even, coup, pltpu.roll(coup, 1, 1))
            det = a * partner - coup * coup
            fa[pl.ds(i * 128, 128), :] = (partner / det).T
            fb[pl.ds(i * 128, 128), :] = (-coup / det).T

    def pivot(v, fa, fb, start, n):
        at = pl.ds(0, n) if n >= 128 else pl.ds(pl.multiple_of(start % 128, n), n)
        a = jnp.concatenate([fa[at, :]] * (W // 128), axis=1)
        b = jnp.concatenate([fb[at, :]] * (W // 128), axis=1)
        even = lax.broadcasted_iota(jnp.int32, (n, W), 0) % 2 == 0
        partner = jnp.where(even, pltpu.roll(v, n - 1, 0), pltpu.roll(v, 1, 0))
        return a * v + b * partner

    def make_coefs():
        coefficients(cdiag, coff, cpat, cfa, cfb, c * pc, pc)
        coefficients(rdiag, roff, rpat, rfa, rfb, me * pr, pr)

    def away(i, size):
        return size // 2 + (1 - 2 * (i % 2)) * ((i + 1) // 2)

    half = CR // 2

    def col_core_send(h, s_a, r_a, st):
        send(s_a.at[h, pl.ds((1 - k) * half, half)], r_a.at[h], snd.at[h, st], rcv.at[h, st], sib)

    def col_y_send(h, s_a, r_a, s_b, r_b, st):
        arrive(r_a.at[h], rcv.at[h, st])
        s_b[h] = (s_a[h, pl.ds(pl.multiple_of(k * half, half), half), :].astype(F32) + r_a[h].astype(F32)).astype(BF)
        for d in [away(n, Y) for n in range(Y - 1)]:
            p = (y + d) % Y
            send(s_b.at[h, pl.ds(p * pc, pc)], r_b.at[h, pl.ds((d - 1) * pc, pc)], snd.at[h, st + 1], rcv.at[h, st + 1], y_id(d))
        sent(r_b.at[h], snd.at[h, st + 1])

    def col_sum(h, s_b, r_b, st):
        arrive(r_b.at[h], rcv.at[h, st + 1])
        acc = s_b[h, pl.ds(pl.multiple_of(y * pc, pc), pc), :].astype(F32)
        for d in range(Y - 1):
            acc = acc + r_b[h, d * pc : (d + 1) * pc, :].astype(F32)
        return acc

    def col_gather(h, buf, value, st, ys):
        at = pl.ds(pl.multiple_of(k * half + y * pc, pc), pc)
        buf[h, at, :] = value
        for d in [away(n, Y) for n in range(Y - 1)]:
            send(buf.at[h, at], buf.at[h, at], snd.at[h, st], ysem.at[h, ys, d - 1], y_id(d))
        send(buf.at[h, at], buf.at[h, at], snd.at[h, st + 1], rcv.at[h, st + 1], sib)
        sent(buf.at[h, pl.ds(0, (Y - 1) * pc)], snd.at[h, st])
        sent(buf.at[h, pl.ds(0, half)], snd.at[h, st + 1])

    def col_forward(h, buf, st, ys):
        for d in (1, Y - 1, 2) if Y == 4 else range(1, Y):
            at = pl.ds(pl.multiple_of(k * half + ((y + Y - d) % Y) * pc, pc), pc)
            arrive(buf.at[h, at], ysem.at[h, ys, d - 1])
            send(buf.at[h, at], buf.at[h, at], snd.at[h, st + 1], rcv.at[h, st + 1], sib)

    def col_gathered(h, buf, st):
        arrive(buf.at[h, pl.ds(0, half)], rcv.at[h, st + 1])

    def far(i):
        return away(i, Z)

    def chip(n):
        return (t + away(n // Y, T)) % T * Y + (y + away(n % Y, Y)) % Y

    def z_scatter(h, s, rr, n, st):
        def step(i, carry):
            d = far(i)
            to = (r + d) % Z
            send(s.at[h, pl.ds(to * n, n)], rr.at[h, pl.ds((d - 1) * n, n)], snd.at[h, st], rcv.at[h, st], z_id(d))
            return carry

        lax.fori_loop(0, Z - 1, step, 0)
        sent(rr.at[h], snd.at[h, st])

    def z_product(h, mat, vec, s, rr, n, st):
        side = Z // 2
        rows = side * n

        def step(i, carry):
            g = (r // side + 1 + i) % 2
            at = pl.multiple_of(g * rows, rows)
            s[h, pl.ds(at, rows), :] = nn(mat[pl.ds(at, rows), :], vec[h]).astype(BF)
            for j in range(side):
                to = g * side + j

                @pl.when(to != r)
                def _():
                    d = (to - r + Z) % Z
                    send(s.at[h, pl.ds(to * n, n)], rr.at[h, pl.ds((d - 1) * n, n)], snd.at[h, st], rcv.at[h, st], (t, to, c))

            return carry

        lax.fori_loop(0, 2, step, 0)
        sent(rr.at[h], snd.at[h, st])

    def z_sum(h, s, rr, n, st):
        arrive(rr.at[h], rcv.at[h, st])
        acc = s[h, pl.ds(pl.multiple_of(r * n, n), n), :].astype(F32)
        for d in range(Z - 1):
            acc = acc + rr[h, d * n : (d + 1) * n, :].astype(F32)
        return acc

    def z_gather(h, buf, value, n, st):
        at = pl.ds(pl.multiple_of(r * n, n), n)
        buf[h, at, :] = value

        def step(i, carry):
            send(buf.at[h, at], buf.at[h, at], snd.at[h, st], rcv.at[h, st], z_id(far(i)))
            return carry

        lax.fori_loop(0, Z - 1, step, 0)
        sent(buf.at[h, pl.ds(0, (Z - 1) * n)], snd.at[h, st])

    def z_gathered(h, buf, n, st):
        arrive(buf.at[h, pl.ds(0, (Z - 1) * n)], rcv.at[h, st])

    def z_tree_scatter(h, s, mid, rr, n, st):
        def part(to):
            return s.at[h, pl.ds(((r + to) % Z) * n, n)]

        for i, (to, via) in enumerate(((3, 1), (Z - 3, Z - 1), (4, (2, Z - 2)[h % 2]))):
            sem = zsem.at[h, 2 + (i if i < 2 else h % 2)]
            send(part(to), mid.at[h, pl.ds(i * n, n)], snd.at[h, st], sem, z_id(via))
        for i, to in enumerate((1, Z - 1)):
            send(part(to), rr.at[h, pl.ds(i * n, n)], snd.at[h, st], rcv.at[h, st], z_id(to))
        sent(s.at[h, pl.ds(0, 5 * n)], snd.at[h, st])

    def z_tree_pass(h, s, mid, rr, n, st):
        for i, to in enumerate((2, Z - 2)):
            both = i == h % 2
            view = mid.at[h, pl.ds(0, (2 if both else 1) * n)]
            arrive(view, zsem.at[h, 2 + i])
            at = pl.ds(pl.multiple_of(((r + to) % Z) * n, n), n)
            acc = s[h, at, :].astype(F32) + mid[h, i * n : (i + 1) * n, :].astype(F32)
            if both:
                acc = acc + mid[h, 2 * n : 3 * n, :].astype(F32)
            s[h, at, :] = acc.astype(BF)
            send(s.at[h, at], rr.at[h, pl.ds((2 + i) * n, n)], snd.at[h, st + 1], rcv.at[h, st], z_id(to))
        sent(s.at[h, pl.ds(0, 2 * n)], snd.at[h, st + 1])

    def z_tree_sum(h, s, rr, n, st):
        arrive(rr.at[h, pl.ds(0, 4 * n)], rcv.at[h, st])
        acc = s[h, pl.ds(pl.multiple_of(r * n, n), n), :].astype(F32)
        for d in range(4):
            acc = acc + rr[h, d * n : (d + 1) * n, :].astype(F32)
        return acc

    def z_tree(h, buf, value, n, st):
        at = pl.ds(pl.multiple_of(r * n, n), n)
        buf[h, at, :] = value
        for i, d in enumerate((2, Z - 2)):
            send(buf.at[h, at], buf.at[h, at], snd.at[h, st], zsem.at[h, i], z_id(d))
        for d in (1, Z - 1):
            send(buf.at[h, at], buf.at[h, at], snd.at[h, st], rcv.at[h, st], z_id(d))
        sent(buf.at[h, pl.ds(0, (Z - 1) * n)], snd.at[h, st])

    def z_tree_forward(h, buf, n, st):
        for i, d in enumerate((2, Z - 2)):
            at = pl.ds(pl.multiple_of(((r + Z - d) % Z) * n, n), n)
            arrive(buf.at[h, at], zsem.at[h, i])
            if i == h % 2:
                send(buf.at[h, at], buf.at[h, at], snd.at[h, st], rcv.at[h, st], z_id(d))
            send(buf.at[h, at], buf.at[h, at], snd.at[h, st], rcv.at[h, st], z_id((1, Z - 1)[i]))

    def exchange(h, mat, vec, s, rr, st):
        per = XT // CAP
        groups = NS // XT

        def step(i, carry):
            g = (me // per + 1 + i) % groups
            at = pl.multiple_of(g * XT, XT)
            s[h, pl.ds(at, XT), :] = nn(mat[pl.ds(at, XT), :], vec[h]).astype(BF)
            for j in range(per):
                q = g * per + j

                @pl.when(q != me)
                def _():
                    send(s.at[h, pl.ds(q * CAP, CAP)], rr.at[h, pl.ds(me * CAP, CAP)], snd.at[h, st], rcv.at[h, st], plane_id(q))

            return carry

        lax.fori_loop(0, groups, step, 0)
        sent(rr.at[h, pl.ds(0, NS - CAP)], snd.at[h, st])
        at = pl.ds(pl.multiple_of(me * CAP, CAP), CAP)
        rr[h, at, :] = s[h, at, :]

    def exchanged(h, rr, st):
        arrive(rr.at[h, pl.ds(0, NS - CAP)], rcv.at[h, st])

    def live(h):
        rows = r * CR + c * pc + lax.broadcasted_iota(jnp.int32, (pc, W), 0)
        return rows < piv[...]

    def b(h):
        col_y_send(h, s1, r1, s2, r2, 0)

    def cc(h):
        acc = col_sum(h, s2, r2, 0)
        solved = jnp.where(live(h), acc, 0.0).astype(BF)
        col_gather(h, sol, solved, 2, 0)

    def d(h):
        col_forward(h, sol, 2, 0)

    def e(h):
        col_gathered(h, sol, 2)
        exchange(h, lst, sol, s3, r3, 4)

    def f(h):
        exchanged(h, r3, 4)
        if ZH:
            z_product(h, asm, r3, s4, r4, pz, 5)
            return

        def fn(i):
            s4[h, pl.ds(i, MT), :] = nn(asm[pl.ds(i, MT), :], r3[h]).astype(BF)

        tiled(RB, fn)
        z_scatter(h, s4, r4, pz, 5)

    def g(h):
        acc = z_sum(h, s4, r4, pz, 5)
        mine = rrhs[pl.ds(pl.multiple_of(r * pz, pz), pz), h * W : (h + 1) * W].astype(F32)
        z_gather(h, upd, (mine - acc).astype(BF), pz, 6)

    def hh(h):
        z_gathered(h, upd, pz, 6)

        def fn(i):
            tile = root[pl.ds(i // pr, MT // pr)].reshape(MT, RB)
            s6[h, pl.ds(i, MT), :] = nn(tile, upd[h]).astype(BF)

        rh = RR // 2
        halves(RR, fn, lambda: send(s6.at[h, pl.ds((1 - k) * rh, rh)], r6.at[h], snd.at[h, 7], rcv.at[h, 7], sib))
        sent(r6.at[h], snd.at[h, 7])

    def i_(h):
        arrive(r6.at[h], rcv.at[h, 7])
        rh = RR // 2
        gi = t * Y + y

        def step(j, carry):
            p = chip(j)
            at = pl.ds(pl.multiple_of(p * pr, pr), pr)
            mine = pl.ds(pl.multiple_of(k * rh + p * pr, pr), pr)
            s6b[h, at, :] = (s6[h, mine, :].astype(F32) + r6[h, at, :].astype(F32)).astype(BF)

            @pl.when(p != gi)
            def _():
                send(s6b.at[h, at], r6b.at[h, pl.ds(j * pr, pr)], snd.at[h, 8], rcv.at[h, 8], g_id(p))

            return carry

        lax.fori_loop(0, G, step, 0)
        sent(r6b.at[h], snd.at[h, 8])

    def j_(h):
        arrive(r6b.at[h], rcv.at[h, 8])
        gi = t * Y + y
        acc = s6b[h, pl.ds(pl.multiple_of(gi * pr, pr), pr), :].astype(F32)
        for n in range(G - 1):
            acc = acc + r6b[h, n * pr : (n + 1) * pr, :].astype(F32)
        value = pivot(acc, rfa, rfb, me * pr, pr).astype(BF)
        at = pl.ds(pl.multiple_of((k * G + gi) * pr, pr), pr)
        rsc[h, at, :] = value

        def step(n, carry):
            send(rsc.at[h, at], rsc.at[h, at], snd.at[h, 9], rcv.at[h, 9], g_id(chip(n - 1)))
            return carry

        lax.fori_loop(1, G, step, 0)
        sent(rsc.at[h, pl.ds(0, (G - 1) * pr)], snd.at[h, 9])

    def k_(h):
        rh = RR // 2
        arrive(rsc.at[h, pl.ds(0, (G - 1) * pr)], rcv.at[h, 9])
        mine = pl.ds(k * rh, rh)
        send(rsc.at[h, mine], rsc.at[h, mine], snd.at[h, 10], rcv.at[h, 10], sib)
        sent(rsc.at[h, pl.ds(0, rh)], snd.at[h, 10])

    def split_product(h, mat, buf, rows, wait):
        mine = pl.ds(pl.multiple_of(k * rows, rows), rows)
        rest = pl.ds(pl.multiple_of((1 - k) * rows, rows), rows)
        part = nn(mat[:, mine], buf[h, mine, :])
        wait()
        return (part + nn(mat[:, rest], buf[h, rest, :])).astype(BF)

    def l_(h):
        rh = RR // 2
        s8[h] = split_product(h, roott, rsc, rh, lambda: arrive(rsc.at[h, pl.ds(0, rh)], rcv.at[h, 10]))
        z_scatter(h, s8, r8, pz, 11)

    def m_(h):
        z_gather(h, rs, z_sum(h, s8, r8, pz, 11).astype(BF), pz, 12)

    def n_(h):
        z_gathered(h, rs, pz, 12)
        exchange(h, asmt, rs, s10, r10, 13)
        out_r[:, h * W : (h + 1) * W] = rs[h].astype(F32)

    def o_(h):
        exchanged(h, r10, 13)

        def fn(i):
            s11[h, pl.ds(i, MT), :] = nn(ls[pl.ds(i, MT), :], r10[h]).astype(BF)

        halves(CR, fn, lambda: col_core_send(h, s11, r11, 14))
        sent(r11.at[h], snd.at[h, 14])

    def p_(h):
        col_y_send(h, s11, r11, s11b, r11b, 14)

    def q_(h):
        acc = col_sum(h, s11b, r11b, 14)
        value = jnp.where(live(h), scaled[h] - acc, 0.0).astype(BF)
        col_gather(h, res, value, 16, 1)

    def r_(h):
        col_forward(h, res, 16, 1)

    def s_(h):
        s13[h] = split_product(h, invt, res, half, lambda: col_gathered(h, res, 16))
        if RST:
            z_tree_scatter(h, s13, mid, r13, pu, 18)
        else:
            z_scatter(h, s13, r13, pu, 18)

    def s2_(h):
        if RST:
            z_tree_pass(h, s13, mid, r13, pu, 18)

    def t_(h):
        gather = z_tree if TREE else z_gather
        gather(h, cs, (z_tree_sum if RST else z_sum)(h, s13, r13, pu, 18).astype(BF), pu, 20)

    def t2_(h):
        if TREE:
            z_tree_forward(h, cs, pu, 20)

    def u_(h):
        arrive(cs.at[h, pl.ds(0, (Z - 3 if TREE else Z - 1) * pu)], rcv.at[h, 20])
        out_c[:, h * W : (h + 1) * W] = cs[h].astype(F32)

    def first(start):
        def fn(i):
            at = pl.multiple_of(start + i, MT)
            value = nn(inv[pl.ds(at // pc, MT // pc)].reshape(MT, CC), rhs[...]).astype(BF)
            for h in range(H):
                s1[h, pl.ds(at, MT), :] = value[:, h * W : (h + 1) * W]

        tiled(half, fn)

    def coefs():
        for n in range(6):
            small_loads[n].wait()
        make_coefs()
        at = pl.ds(pl.multiple_of(k * half + y * pc, pc), pc)
        for h in range(H):
            scaled[h] = pivot(sol[h, at, :].astype(F32), cfa, cfb, c * pc, pc)

    small_loads[6].wait()
    make_slots()
    for n in range(3):
        loads[n].wait()
    mask_child()
    first((1 - k) * half)
    small_loads[7].wait()
    pl.semaphore_wait(barrier, Q - 1 + Z - 1)
    for h in range(H):
        col_core_send(h, s1, r1, 0)
        sent(r1.at[h], snd.at[h, 0])
    first(k * half)
    local = {
        "sel": make_sel,
        "meta": send_meta,
        "lst0": lambda: make_lst(0),
        "lst1": lambda: make_lst(1),
        "ident": make_ident,
        "asm": make_asm,
        "coefs": coefs,
        "mask": mask_root,
        "roott": lambda: transpose_into(root, roott, RR, RB, pr),
        "ls0": lambda: make_ls(0),
        "ls1": lambda: make_ls(1),
        "asmt": make_asmt,
        "invt": lambda: transpose_into(inv, invt, CR, CC, pc),
        "rrhs": loads[7].wait,
    }
    steps = [b, cc, d, e, f, g, hh, i_, j_, k_, l_, m_, n_, o_, p_, q_, r_, s_, s2_, t_, t2_, u_]
    names = dict(zip("bcdefghijklmnopqrsStTu", steps))
    for item in ORDER:
        if item in local:
            local[item]()
        else:
            names[item[0]](int(item[1]))
    for view, sem in pending:
        arrive(view, sem)


def shards(dims, *args):
    (child_inverse, child_lower, child_rhs, child_diag, child_off, child_pattern, child_pivots, child_map,
     root_inverse, root_rhs, root_diag, root_off, root_pattern) = args
    T, Z, Y, CR, CC, U, RB, RR, R, H = dims
    C, Q, G, W = Y * CORES, T * Y * CORES, T * Y, R // H
    NS = Q * CAP
    pc, pr, pz, pu = CR // C, RR // Q, RB // Z, CC // Z

    def chain(rows):
        return pltpu.VMEM((H, rows, W), BF)

    vm = lambda *shape: pltpu.VMEM(shape, BF)
    fm = lambda *shape: pltpu.VMEM(shape, F32)
    half = CR // 2
    scratch = [
        vm(C, pc, CC), vm(CC, CR), vm(C, pc, U), vm(NS, CR), vm(CR, NS), vm(NS, U), vm(Q, pr, RB), vm(RB, RR),
        vm(RB, NS), vm(NS, RB), vm(TILE, TILE), vm(CC, R), vm(RB, R),
        pltpu.VMEM((8, U), jnp.int32), fm(Q // 2, 8, 128), fm(Q, 8, 128),
        fm(max(pc, 128), 128), fm(max(pc, 128), 128), fm(max(pr, 128), 128), fm(max(pr, 128), 128), fm(H, pc, W),
        chain(CR), chain(half), chain(half), chain((Y - 1) * pc), chain(CR), chain(NS), chain(NS), chain(RB),
        chain((Z - 1) * pz), chain(RB),
        chain(RR), chain(RR // 2), chain(RR // 2), chain((G - 1) * pr), chain(RR), chain(RB), chain((Z - 1) * pz),
        chain(RB), chain(NS), chain(NS),
        chain(CR), chain(half), chain(half), chain((Y - 1) * pc), chain(CR), chain(CC), chain((Z - 1) * pu), chain(3 * pu), chain(CC),
        *[pltpu.VMEM((1, n), dt) for n, dt in ((CR, F32), (CR, F32), (CR, jnp.int32), (RR, F32), (RR, F32), (RR, jnp.int32), (U, jnp.int32), (1, jnp.int32))],
        pltpu.SemaphoreType.DMA((8,)), pltpu.SemaphoreType.DMA((8,)), pltpu.SemaphoreType.DMA((H, 21)), pltpu.SemaphoreType.DMA((H, 21)),
        pltpu.SemaphoreType.DMA((H, 2, Y - 1)), pltpu.SemaphoreType.DMA((H, 4)), pltpu.SemaphoreType.DMA((2,)),
    ]
    anyspec = pl.BlockSpec(memory_space=pl.ANY)
    vspec = pl.BlockSpec(memory_space=pltpu.VMEM)
    flops = 2 * R * (2 * CR * CC + 2 * NS * CR + 2 * RB * NS + 2 * RR * RB)
    child, rooted = pl.pallas_call(
        functools.partial(body, dims),
        name="substitution",
        out_shape=(OUT((CC, R), F32), OUT((RB, R), F32)),
        in_specs=[anyspec] * 13,
        out_specs=(vspec, vspec),
        scratch_shapes=scratch,
        cost_estimate=pl.CostEstimate(flops=flops, bytes_accessed=8 << 20, transcendentals=0),
        compiler_params=pltpu.CompilerParams(collective_id=0, has_side_effects=True, vmem_limit_bytes=58 << 20),
    )(
        child_inverse.reshape(Y, CORES, pc, CC),
        child_lower.reshape(Y, CORES, pc, U),
        root_inverse.reshape(G, CORES, pr, RB),
        child_rhs.reshape(CC, R),
        root_rhs,
        child_diag.reshape(1, CR),
        child_off.reshape(1, CR),
        child_pattern.reshape(1, CR),
        root_diag.reshape(1, RR),
        root_off.reshape(1, RR),
        root_pattern.reshape(1, RR),
        child_map.reshape(1, U),
        child_pivots.reshape(1, 1),
    )
    return (child[None], rooted)


def solution(mesh):
    T, Z, C = mesh.shape["team"], mesh.shape["row"], mesh.shape["col"]

    def run(*args):
        pc_, uc = args[0].shape[1], args[1].shape[2]
        fr, R = args[9].shape
        dims = (T, Z, C // CORES, pc_ // Z, pc_ // C, uc // C, fr // (T * C), fr // Z, R, CHAINS)
        return jax.shard_map(
            functools.partial(shards, dims),
            mesh=mesh,
            in_specs=(
                P("team", "row", "col"),
                P("team", "row", "col"),
                P("team", "col", None),
                P("team", "row"),
                P("team", "row"),
                P("team", "row"),
                P("team"),
                P("team", "col"),
                P("row", ("team", "col")),
                P(("team", "col"), None),
                P("row"),
                P("row"),
                P("row"),
            ),
            out_specs=(P("team", "col", None), P(("team", "col"), None)),
            check_vma=False,
        )(*args)

    return run
```
